128 devices in a mesh: wide: 16 (over y, x), narrow: 8 (over z, core).
Axes of the slice: x: 4, y: 4, z: 4, core: 2. Of those that a mesh axis runs over, the one named last changes fastest.
Arguments:
- amplitudes: bfloat16 [8, 2048, 2048], P(None, ('wide', 'narrow')), may hold values from -6 to 6
- df_factor: bfloat16 [8, 2048, 2048], P(None, 'wide', 'narrow'), may hold values from -0.0625 to 0.0625
- amp_mask: int32 [16, 16], replicated, may hold values 0 or 1
- factor_mask: int32 [16, 16], replicated, may hold values 0 or 1
Outputs:
- ladder: float32 [8, 2048, 2048], P(None, 'wide', 'narrow')
The draws below stay inside these ranges and needn't reach their ends.
All inputs are finite; a program needn't handle non-finite values.
Results may differ from the reference program's by a relative error of at most 0.0029.
Values may be sent and summed in bfloat16 or wider, within the bound.
A program may use at most 128 MiB of HBM per device.

```python
import jax
import jax.numpy as jnp
from jax import lax

PAIRS = 8
V = 2048
TILE = 128
NAUXB = 8
NT = 16


def with_ends(drawn, rng, low, high):
    longest = drawn.shape.index(max(drawn.shape))
    spots = []
    for shift in (0, 1):
        where = [jax.random.randint(jax.random.fold_in(rng, axis), (), 0, length) for axis, length in enumerate(drawn.shape)]
        where[longest] = (where[longest] + shift) % drawn.shape[longest]
        spots.append(tuple(where))
    return drawn.at[spots[0]].set(low).at[spots[1]].set(high)


def block_scale(own_key, extent, shards, low, largest):
    loudness, own = 1.0, jax.random.fold_in(own_key, 6)
    for axis_at, shards_of in shards:
        draws = jnp.exp(jax.random.uniform(jax.random.fold_in(own, axis_at), (shards_of,), jnp.float32, low / len(shards), largest / len(shards)))
        loudness = loudness * jnp.repeat(draws, extent[axis_at] // shards_of).reshape([-1 if axis == axis_at else 1 for axis in range(len(extent))])
    return loudness


def gaussian(own_key, shape, spread, limit, shards=(), kind=jnp.bfloat16):
    drawn = jax.random.normal(own_key, shape, jnp.float32) * spread
    if len(shards) > 0:
        drawn = block_scale(own_key, shape, shards, -0.22, 0.18) * drawn
    return jnp.clip(drawn, min=-limit, max=limit).astype(kind)


def setup_inputs(seed: int = 0) -> dict:
    arg_keys = jax.random.split(jax.random.key(seed), 5)
    return {
        "amplitudes": gaussian(arg_keys[0], (PAIRS, V, V), 1.0, 6.0, ((1, 128),)),
        "df_factor": gaussian(arg_keys[1], (NAUXB, V, V), (4 * V) ** -0.5, 0.0625, ((1, 16), (2, 8))),
        "amp_mask": with_ends((jax.random.randint(arg_keys[2], (NT, NT), 0, 4) < 3).astype(jnp.int32), jax.random.fold_in(arg_keys[2], 1), 0, 1),
        "factor_mask": with_ends((jax.random.randint(arg_keys[3], (NT, NT), 0, 4) < 3).astype(jnp.int32), jax.random.fold_in(arg_keys[3], 1), 0, 1),
    }


def expand(mask):
    tiles = (jnp.arange(V) // TILE).astype(jnp.int32)
    return mask[tiles][:, tiles]


def reference(amplitudes, df_factor, amp_mask, factor_mask):
    amps = amplitudes * expand(amp_mask).astype(jnp.bfloat16)[None]
    factor = df_factor * expand(factor_mask).astype(jnp.bfloat16)[None]
    factor_wide = factor.astype(jnp.float32)

    def one_pair(pair_amps):
        halfway = jnp.einsum("pac,cd->pad", factor_wide, pair_amps.astype(jnp.float32))
        halfway = halfway.astype(jnp.bfloat16).astype(jnp.float32)
        return jnp.einsum("pad,pbd->ab", halfway, factor_wide)

    return lax.map(one_pair, amps)
```

```python
import functools

import jax
import jax.numpy as jnp
from jax import lax
from jax.experimental import pallas as pl
from jax.experimental.pallas import tpu as pltpu
from jax.sharding import PartitionSpec as P

MESH = pl.DeviceIdType.MESH
BF16 = jnp.bfloat16
F32 = jnp.float32
TRANSPOSED = (((1,), (1,)), ((), ()))

LAG = 2.0
FACTOR_CHUNKS = 8
PAIRS = 8


def kernel(amp_ref, fac_ref, amask, fmask, out_ref, tsrc, fsrc, g2, fr, half, part, ring_in, comb, quad, fin, pin, pp,
           g_recv, g_send, f_recv, f_send, e_send, a_recv, a_send, o_recv, o_send, q_send):
    w, n = lax.axis_index("wide"), lax.axis_index("narrow")
    y, x = w // 4, w % 4
    z, c = n // 2, n % 2
    A, xl = x // 2, x % 2
    D = ((x + 1) // 2) % 2
    up = lambda v, s: lax.rem(v + s + 4, 4)
    x_of = lambda a, d: a * 3 + d * (1 - 2 * a)
    dev = lambda yy, xx, zz, cc: (yy * 4 + xx, zz * 2 + cc)
    z1, z2, z3 = up(z, 1), up(z, 2), up(z, 3)
    y1, y2, y3 = up(y, 1), up(y, 2), up(y, 3)
    z_up, z_down = dev(y, x, z1, c), dev(y, x, z3, c)
    y_up, y_down = dev(y1, x, z, c), dev(y3, x, z, c)
    a_pair = dev(y, x_of(1 - A, D), z, c)
    d_pair = dev(y, x_of(A, 1 - D), z, c)
    sibling = dev(y, x, z, 1 - c)
    on_home_chip = x == 2 * A + c

    def push(src, dst, send, recv, to):
        pltpu.make_async_remote_copy(src_ref=src, dst_ref=dst, send_sem=send, recv_sem=recv, device_id=to, device_id_type=MESH).start()

    def push_or_copy(here, src, dst, send, recv, to):
        @pl.when(here)
        def _():
            pltpu.make_async_copy(src, dst, recv).start()

        @pl.when(jnp.logical_not(here))
        def _():
            push(src, dst, send, recv, to)

    def wait(ref, sem):
        pltpu.make_async_copy(ref, ref, sem).wait()

    def units(count):
        return g2.at[pl.ds(0, count), 0, 0, 0]

    barrier = pltpu.get_barrier_semaphore()
    for dz in range(4):
        for dd in range(2):
            for dc in range(2):
                if dz or dd or dc:
                    xx = x_of(A, D if dd == 0 else 1 - D)
                    cc = c if dc == 0 else 1 - c
                    pl.semaphore_signal(barrier, inc=1, device_id=dev(y, xx, up(z, dz), cc), device_id_type=MESH)
    for to in (y_up, y_down, a_pair):
        pl.semaphore_signal(barrier, inc=1, device_id=to, device_id_type=MESH)

    for h in range(2):
        keep = fmask[w, 2 * n + h].astype(F32)
        cols = pl.ds(h * 128, 128)
        fsrc[:, :, cols] = (fac_ref[:, :, cols].astype(F32) * keep).astype(BF16)
    for h in range(16):
        keep = amask[w, h].astype(F32)
        cols = pl.ds(h * 128, 128)
        tsrc[:, :, cols] = (amp_ref[:, :, cols].astype(F32) * keep).astype(BF16)

    pl.semaphore_wait(barrier, 18)

    ends = []

    for k in range(FACTOR_CHUNKS):
        for d in range(2):
            here = jnp.logical_and(x_of(A, d) == x, xl == c)
            wanted = None if k % 2 == 0 else c == d

            def go(k=k, d=d, here=here):
                push_or_copy(here, fsrc.at[k], fr.at[k, z, c], e_send.at[k, d], f_recv.at[k, 5], dev(y, x_of(A, d), z, xl))

            if wanted is None:
                go()
            else:
                pl.when(wanted)(go)
            sent = jnp.logical_not(here) if wanted is None else jnp.logical_and(wanted, jnp.logical_not(here))
            ends.append(lambda k=k, d=d, sent=sent: pl.when(sent)(lambda: wait(fsrc.at[k], e_send.at[k, d])))

    for dz in range(4):
        for d in range(2):
            zz = up(z, dz)
            here = jnp.logical_and(jnp.logical_and(x_of(A, d) == x, xl == c), dz == 0)
            cols = pl.ds(pl.multiple_of((2 * zz + d) * 256, 256), 256)
            rows = pl.ds(pl.multiple_of((2 * z + c) * 16, 16), 16)
            src = tsrc.at[:, :, cols]
            dst = g2.at[pl.ds(8, 8), y, A, xl, rows]
            if dz == 0:
                push_or_copy(here, src, dst, a_send.at[dz, d], a_recv.at[0], dev(y, x_of(A, d), zz, xl))
                ends.append(lambda src=src, dz=dz, d=d, here=here: pl.when(jnp.logical_not(here))(lambda: wait(src, a_send.at[dz, d])))
            else:
                push(src, dst, a_send.at[dz, d], a_recv.at[0], dev(y, x_of(A, d), zz, xl))
                ends.append(lambda src=src, dz=dz, d=d: wait(src, a_send.at[dz, d]))

    lo, hi = pl.ds(0, 64), pl.ds(64, 64)

    def f1(k):
        if k % 2 == 0:
            wait(fr.at[k, z], f_recv.at[k, 5])
        else:
            wait(fr.at[k, z, D], f_recv.at[k, 5])
        g2[k, y, A, c] = fr[k, z, D]
        own = fr.at[k, z] if k % 2 == 0 else fr.at[k, z, D]
        push(own, own, f_send.at[k], f_recv.at[k, 0], z_up)
        push(own, own, f_send.at[k], f_recv.at[k, 1], z_down)
        if k % 2:
            push(own, own, f_send.at[k], f_recv.at[k, 4], d_pair)

    def f2(k):
        if k % 2 == 0:
            wait(fr.at[k, z3], f_recv.at[k, 0])
            push(fr.at[k, z3, 0], fr.at[k, z3, 0], f_send.at[k], f_recv.at[k, 2], z_up)
            wait(fr.at[k, z1], f_recv.at[k, 1])
            push(fr.at[k, z1, 1], fr.at[k, z1, 1], f_send.at[k], f_recv.at[k, 3], z_down)
        else:
            wait(fr.at[k, z3, D], f_recv.at[k, 0])
            push(fr.at[k, z3, D, lo], fr.at[k, z3, D, lo], f_send.at[k], f_recv.at[k, 2], z_up)
            push(fr.at[k, z3, D], fr.at[k, z3, D], f_send.at[k], f_recv.at[k, 4], d_pair)
            wait(fr.at[k, z1, D], f_recv.at[k, 1])
            push(fr.at[k, z1, D, hi], fr.at[k, z1, D, hi], f_send.at[k], f_recv.at[k, 3], z_down)
            push(fr.at[k, z1, D], fr.at[k, z1, D], f_send.at[k], f_recv.at[k, 4], d_pair)

    def f3(k):
        if k % 2 == 0:
            wait(fr.at[k, z2, 0], f_recv.at[k, 2])
            wait(fr.at[k, z2, 1], f_recv.at[k, 3])
            ends.append(lambda: wait(units(6), f_send.at[k]))
        else:
            wait(fr.at[k, z2, D, lo], f_recv.at[k, 2])
            wait(fr.at[k, z2, D, hi], f_recv.at[k, 3])
            push(fr.at[k, z2, D], fr.at[k, z2, D], f_send.at[k], f_recv.at[k, 4], d_pair)
            ends.append(lambda: wait(units(7), f_send.at[k]))

    def f4(k):
        if k % 2:
            wait(fr.at[k, :, 1 - D], f_recv.at[k, 4])

    def s1(k):
        own = g2.at[k, y, A, c]
        if k == 8:
            wait(g2.at[pl.ds(8, 8), y, A, c], a_recv.at[0])
        if k % 2 == 0:
            push(own, own, g_send.at[k], g_recv.at[k, 4], a_pair)
        else:
            push(own, own, g_send.at[k], g_recv.at[k, 0], y_up)
            push(own, own, g_send.at[k], g_recv.at[k, 1], y_down)
            push(own, own, g_send.at[k], g_recv.at[k, 4], a_pair)

    def s2(k):
        if k % 2 == 0:
            wait(g2.at[k, y, 1 - A, c], g_recv.at[k, 4])
            own = g2.at[k, y, :, c]
            push(own, own, g_send.at[k], g_recv.at[k, 0], y_up)
            push(own, own, g_send.at[k], g_recv.at[k, 1], y_down)
        else:
            b = g2.at[k, y3, A, c]
            wait(b, g_recv.at[k, 0])
            push(b.at[lo], b.at[lo], g_send.at[k], g_recv.at[k, 2], y_up)
            push(b, b, g_send.at[k], g_recv.at[k, 4], a_pair)
            b = g2.at[k, y1, A, c]
            wait(b, g_recv.at[k, 1])
            push(b.at[hi], b.at[hi], g_send.at[k], g_recv.at[k, 3], y_down)
            push(b, b, g_send.at[k], g_recv.at[k, 4], a_pair)

    def s3(k):
        if k % 2 == 0:
            wait(g2.at[k, y3, :, c], g_recv.at[k, 0])
            push(g2.at[k, y3, 0, c], g2.at[k, y3, 0, c], g_send.at[k], g_recv.at[k, 2], y_up)
            wait(g2.at[k, y1, :, c], g_recv.at[k, 1])
            push(g2.at[k, y1, 1, c], g2.at[k, y1, 1, c], g_send.at[k], g_recv.at[k, 3], y_down)
        else:
            b = g2.at[k, y2, A, c]
            wait(b.at[lo], g_recv.at[k, 2])
            wait(b.at[hi], g_recv.at[k, 3])
            push(b, b, g_send.at[k], g_recv.at[k, 4], a_pair)

    def s4(k):
        if k % 2 == 0:
            wait(g2.at[k, y2, 0, c], g_recv.at[k, 2])
            wait(g2.at[k, y2, 1, c], g_recv.at[k, 3])
        else:
            wait(g2.at[k, :, 1 - A, c], g_recv.at[k, 4])
        mine = g2.at[k, :, :, c]
        push(mine, mine, g_send.at[k], g_recv.at[k, 5], sibling)
        ends.append(lambda: wait(units(15), g_send.at[k]))

    def s5(k):
        wait(g2.at[k, :, :, 1 - c], g_recv.at[k, 5])

    def halfway(i):
        for q in range(2):
            acc = jnp.zeros((512, 256), F32)
            for m in range(8):
                rows = fr[pl.ds(4 * q, 4), m // 2, m % 2].reshape(512, 256)
                acc += jnp.dot(rows, g2[8 + i, m // 2, m % 2].reshape(256, 256), preferred_element_type=F32)
            half[pl.ds(4 * q, 4), pl.ds((i % 2) * 128, 128)] = acc.astype(BF16).reshape(4, 128, 256)

    def ladder(j, q):
        acc = jnp.zeros((256, 1024), F32)
        for p in range(8):
            acc += lax.dot_general(half[p], g2[p, pl.ds(2 * q, 2)].reshape(1024, 256), TRANSPOSED, preferred_element_type=F32)
        acc = acc.astype(BF16)
        for h in range(2):
            for m in range(4):
                part[2 * j + h, 2 * q + m // 2, m % 2] = acc[h * 128:(h + 1) * 128, m * 256:(m + 1) * 256]

    add = lambda *terms: functools.reduce(lambda a, b: a + b, [t.astype(F32) for t in terms])

    def owner_push(i, src_of, dst, sem):
        for cc in range(2):
            here = jnp.logical_and(on_home_chip, c == cc)
            src = src_of(cc)
            push_or_copy(here, src, dst, q_send.at[i, cc], sem, dev(y, 2 * A + c, z, cc))
            ends.append(lambda src=src, cc=cc, here=here: pl.when(jnp.logical_not(here))(lambda: wait(src, q_send.at[i, cc])))

    def scatter_first(i, block, first, second):
        send = o_send.at[i]
        rin = ring_in.at[i]
        push(block(z2).at[first], rin.at[0, first], send, o_recv.at[i, 0], z_up)
        push(block(z2, 1).at[second], rin.at[0, second] if i % 2 else rin.at[3, second], send, o_recv.at[i, 1], z_down)
        push(block(z3).at[first], rin.at[1, first], send, o_recv.at[i, 2], z_down)
        push(block(z1, 1).at[second], rin.at[1, second] if i % 2 else rin.at[4, second], send, o_recv.at[i, 3], z_up)

    def o1(i):
        if i % 2 == 0:
            block = lambda zz, d=0: part.at[i, zz, d]
            scatter_first(i, block, pl.ds(0, 128), pl.ds(0, 128))
        else:
            owner_push(i, lambda cc: part.at[i, :, cc], pin.at[i // 2, D], o_recv.at[i, 4])

    def o2(i):
        rin = ring_in.at[i]
        if i % 2 == 0:
            wait(rin.at[0], o_recv.at[i, 0])
            comb[i, 0] = add(part[i, z1, 0], ring_in[i, 0]).astype(BF16)
            push(comb.at[i, 0], rin.at[2], o_send.at[i], o_recv.at[i, 2], z_up)
            wait(rin.at[3], o_recv.at[i, 1])
            comb[i, 1] = add(part[i, z3, 1], ring_in[i, 3]).astype(BF16)
            push(comb.at[i, 1], rin.at[5], o_send.at[i], o_recv.at[i, 3], z_down)
        else:
            j = i // 2
            wait(pin.at[j], o_recv.at[i, 4])
            pp[j] = add(pin[j, 0], pin[j, 1]).astype(BF16)
            scatter_first(i, lambda zz, d=0: pp.at[j, zz], lo, hi)

    def o3(i):
        rin = ring_in.at[i]
        if i % 2 == 0:
            wait(rin.at[pl.ds(1, 2)], o_recv.at[i, 2])
            wait(rin.at[pl.ds(4, 2)], o_recv.at[i, 3])
            quad[i // 2, 0] = add(part[i, z, 0], ring_in[i, 1], ring_in[i, 2]).astype(BF16)
            quad[i // 2, 1] = add(part[i, z, 1], ring_in[i, 4], ring_in[i, 5]).astype(BF16)
            owner_push(i, lambda cc: quad.at[i // 2, cc], fin.at[i // 2, D], o_recv.at[i, 4])
            ends.append(lambda: wait(units(6), o_send.at[i]))
        else:
            j = i // 2
            wait(rin.at[0, lo], o_recv.at[i, 0])
            comb[i, 0, lo] = add(pp[j, z1, lo], ring_in[i, 0, lo]).astype(BF16)
            push(comb.at[i, 0, lo], rin.at[2, lo], o_send.at[i], o_recv.at[i, 2], z_up)
            wait(rin.at[0, hi], o_recv.at[i, 1])
            comb[i, 0, hi] = add(pp[j, z3, hi], ring_in[i, 0, hi]).astype(BF16)
            push(comb.at[i, 0, hi], rin.at[2, hi], o_send.at[i], o_recv.at[i, 3], z_down)
            ends.append(lambda: wait(units(3), o_send.at[i]))

    def o4(i):
        j = i // 2
        if i % 2 == 0:
            wait(fin.at[j], o_recv.at[i, 4])
            out_ref[i] = add(fin[j, 0], fin[j, 1])
        else:
            rin = ring_in.at[i]
            wait(rin.at[pl.ds(1, 2), lo], o_recv.at[i, 2])
            wait(rin.at[pl.ds(1, 2), hi], o_recv.at[i, 3])
            out_ref[i] = add(pin[j, 0, z], pin[j, 1, z], ring_in[i, 1], ring_in[i, 2])

    plan = []

    def at(when, step, *args):
        plan.append((when, len(plan), step, args))

    for k in range(FACTOR_CHUNKS):
        for s, step in enumerate((f1, f2, f3, f4)):
            at(k + s * LAG, step, k)
    for k in range(16):
        for s, step in enumerate((s1, s2, s3, s4, s5)):
            at(k + s * LAG + 0.01, step, k)
    for j in range(PAIRS // 2):
        ready = 8 + 2 * j + 1 + 4 * LAG + 0.02
        at(ready - 1, halfway, 2 * j)
        at(ready, halfway, 2 * j + 1)
        at(ready + 0.3, ladder, j, 0)
        at(ready + 0.6, ladder, j, 1)
        for i in (2 * j + 1, 2 * j):
            for s, step in enumerate((o1, o2, o3, o4)):
                at(ready + 0.7 + 0.6 * s, step, i)
    for _, _, step, args in sorted(plan, key=lambda p: (p[0], p[1])):
        step(*args)
    for end in ends:
        end()


def shards(amplitudes, df_factor, amp_mask, factor_mask):
    vmem, smem = pl.BlockSpec(memory_space=pltpu.VMEM), pl.BlockSpec(memory_space=pltpu.SMEM)
    block = lambda *lead: pltpu.VMEM((*lead, 128, 256), BF16)
    dma = lambda *shape: pltpu.SemaphoreType.DMA(shape)
    return pl.pallas_call(
        kernel,
        out_shape=jax.ShapeDtypeStruct((8, 128, 256), F32),
        in_specs=[vmem, vmem, smem, smem],
        out_specs=vmem,
        scratch_shapes=[
            pltpu.VMEM((8, 16, 2048), BF16),
            block(8),
            block(16, 4, 2, 2),
            block(8, 4, 2),
            pltpu.VMEM((8, 256, 256), BF16),
            block(8, 4, 2),
            block(8, 6),
            block(8, 2),
            block(4, 2),
            block(4, 2),
            block(4, 2, 4),
            block(4, 4),
            dma(16, 6), dma(16), dma(8, 6), dma(8), dma(8, 2), dma(1), dma(4, 2), dma(8, 5), dma(8), dma(8, 2),
        ],
        compiler_params=pltpu.CompilerParams(collective_id=0, has_side_effects=True, vmem_limit_bytes=60 * 2**20),
        cost_estimate=pl.CostEstimate(flops=17179869184, bytes_accessed=4 * 2**20, transcendentals=0),
    )(amplitudes, df_factor, amp_mask, factor_mask)


def solution(mesh):
    return jax.shard_map(
        shards,
        mesh=mesh,
        in_specs=(P(None, ("wide", "narrow"), None), P(None, "wide", "narrow"), P(), P()),
        out_specs=P(None, "wide", "narrow"),
        check_vma=False,
    )
```

```python
import functools
import heapq

import jax
import jax.numpy as jnp
from jax import lax
from jax.experimental import pallas as pl
from jax.experimental.pallas import tpu as pltpu
from jax.sharding import PartitionSpec as P

MESH = pl.DeviceIdType.MESH
BF16 = jnp.bfloat16
F32 = jnp.float32
TRANSPOSED = (((1,), (1,)), ((), ()))

SUB = 2
ROWS = 128 // SUB
FACTOR_LAG = 3.0
AMP_LAG = 3.0
CORE_LAG = 1.0
OUT_LAG = 4.0
AHEAD = 4
SHARE_AT = 2.0
READY = 0.0
END_LAG = 8.0


def kernel(amp_ref, fac_ref, amask, fmask, out_ref, tsrc, fsrc, g2, fr, half, part, part32, ring_in, comb, quad, fin, pin, pp,
           g_recv, g_send, f_recv, f_send, e_send, a_recv, a_send, o_recv, o_send, q_send):
    w, n = lax.axis_index("wide"), lax.axis_index("narrow")
    y, x = w // 4, w % 4
    z, c = n // 2, n % 2
    A, xl = x // 2, x % 2
    D = ((x + 1) // 2) % 2
    up = lambda v, s: lax.rem(v + s + 4, 4)
    x_of = lambda a, d: a * 3 + d * (1 - 2 * a)
    dev = lambda yy, xx, zz, cc: (yy * 4 + xx, zz * 2 + cc)
    z1, z2, z3 = up(z, 1), up(z, 2), up(z, 3)
    y1, y2, y3 = up(y, 1), up(y, 2), up(y, 3)
    z_up, z_down = dev(y, x, z1, c), dev(y, x, z3, c)
    y_up, y_down = dev(y1, x, z, c), dev(y3, x, z, c)
    a_pair = dev(y, x_of(1 - A, D), z, c)
    d_pair = dev(y, x_of(A, 1 - D), z, c)
    sibling = dev(y, x, z, 1 - c)
    on_home_chip = x == 2 * A + c

    def push(src, dst, send, recv, to):
        pltpu.make_async_remote_copy(src_ref=src, dst_ref=dst, send_sem=send, recv_sem=recv, device_id=to, device_id_type=MESH).start()

    def push_or_copy(here, src, dst, send, recv, to):
        @pl.when(here)
        def _():
            pltpu.make_async_copy(src, dst, recv).start()

        @pl.when(jnp.logical_not(here))
        def _():
            push(src, dst, send, recv, to)

    def wait(ref, sem):
        pltpu.make_async_copy(ref, ref, sem).wait()

    def units(count):
        return g2.at[pl.ds(0, count), 0, 0, 0, pl.ds(0, ROWS)]

    def split(q):
        k, first = q // SUB, (q % SUB) * ROWS
        return k, q % 2 == 0 or q % 16 == 15, pl.ds(first, ROWS), pl.ds(first, ROWS // 2), pl.ds(first + ROWS // 2, ROWS // 2)

    barrier = pltpu.get_barrier_semaphore()
    for dz in range(4):
        for dd in range(2):
            for dc in range(2):
                if dz or dd or dc:
                    xx = x_of(A, D if dd == 0 else 1 - D)
                    cc = c if dc == 0 else 1 - c
                    pl.semaphore_signal(barrier, inc=1, device_id=dev(y, xx, up(z, dz), cc), device_id_type=MESH)
    for to in (y_up, y_down, a_pair):
        pl.semaphore_signal(barrier, inc=1, device_id=to, device_id_type=MESH)

    for h in range(2):
        keep = fmask[w, 2 * n + h].astype(F32)
        cols = pl.ds(h * 128, 128)
        fsrc[:, :, cols] = (fac_ref[:, :, cols].astype(F32) * keep).astype(BF16)
    for h in range(16):
        keep = amask[w, h].astype(F32)
        cols = pl.ds(h * 128, 128)
        tsrc[:, :, cols] = (amp_ref[:, :, cols].astype(F32) * keep).astype(BF16)

    pl.semaphore_wait(barrier, 18)

    plan = []
    now = [-100.0, 0]

    def at(when, order, step, *args):
        now[1] += 1
        heapq.heappush(plan, (when, order, now[1], step, args))

    def finish(step):
        at(now[0] + END_LAG, 30, step)

    def e1(q):
        k, pair_first, rows, _, _ = split(q)
        for d in range(2):
            here = jnp.logical_and(x_of(A, d) == x, xl == c)

            def go(d=d, here=here):
                push_or_copy(here, fsrc.at[k, rows], fr.at[k, z, c, rows], e_send.at[q, d], f_recv.at[q, 5], dev(y, x_of(A, d), z, xl))

            if pair_first:
                go()
            else:
                pl.when(c == d)(go)
            sent = jnp.logical_not(here) if pair_first else jnp.logical_and(c == d, jnp.logical_not(here))
            finish(lambda d=d, sent=sent: pl.when(sent)(lambda: wait(fsrc.at[k, rows], e_send.at[q, d])))

    def share_amplitudes():
        for dz in range(4):
            for d in range(2):
                zz = up(z, dz)
                here = jnp.logical_and(jnp.logical_and(x_of(A, d) == x, xl == c), dz == 0)
                cols = pl.ds(pl.multiple_of((2 * zz + d) * 256, 256), 256)
                rows = pl.ds(pl.multiple_of((2 * z + c) * 16, 16), 16)
                src = tsrc.at[:, :, cols]
                dst = g2.at[pl.ds(8, 8), y, A, xl, rows]
                if dz == 0:
                    push_or_copy(here, src, dst, a_send.at[dz, d], a_recv.at[0], dev(y, x_of(A, d), zz, xl))
                    finish(lambda src=src, dz=dz, d=d, here=here: pl.when(jnp.logical_not(here))(lambda: wait(src, a_send.at[dz, d])))
                else:
                    push(src, dst, a_send.at[dz, d], a_recv.at[0], dev(y, x_of(A, d), zz, xl))
                    finish(lambda src=src, dz=dz, d=d: wait(src, a_send.at[dz, d]))

    def f1(q):
        k, pair_first, rows, _, _ = split(q)
        own = fr.at[k, z, :, rows] if pair_first else fr.at[k, z, D, rows]
        wait(own, f_recv.at[q, 5])
        g2[k, y, A, c, rows] = fr[k, z, D, rows]
        push(own, own, f_send.at[q], f_recv.at[q, 0], z_up)
        push(own, own, f_send.at[q], f_recv.at[q, 1], z_down)
        if not pair_first:
            push(own, own, f_send.at[q], f_recv.at[q, 4], d_pair)

    def f2(q):
        k, pair_first, rows, lo, hi = split(q)
        if pair_first:
            wait(fr.at[k, z3, :, rows], f_recv.at[q, 0])
            push(fr.at[k, z3, 0, rows], fr.at[k, z3, 0, rows], f_send.at[q], f_recv.at[q, 2], z_up)
            wait(fr.at[k, z1, :, rows], f_recv.at[q, 1])
            push(fr.at[k, z1, 1, rows], fr.at[k, z1, 1, rows], f_send.at[q], f_recv.at[q, 3], z_down)
        else:
            wait(fr.at[k, z3, D, rows], f_recv.at[q, 0])
            push(fr.at[k, z3, D, lo], fr.at[k, z3, D, lo], f_send.at[q], f_recv.at[q, 2], z_up)
            push(fr.at[k, z3, D, rows], fr.at[k, z3, D, rows], f_send.at[q], f_recv.at[q, 4], d_pair)
            wait(fr.at[k, z1, D, rows], f_recv.at[q, 1])
            push(fr.at[k, z1, D, hi], fr.at[k, z1, D, hi], f_send.at[q], f_recv.at[q, 3], z_down)
            push(fr.at[k, z1, D, rows], fr.at[k, z1, D, rows], f_send.at[q], f_recv.at[q, 4], d_pair)

    def f3(q):
        k, pair_first, rows, lo, hi = split(q)
        if pair_first:
            wait(fr.at[k, z2, 0, rows], f_recv.at[q, 2])
            wait(fr.at[k, z2, 1, rows], f_recv.at[q, 3])
            finish(lambda: wait(units(6), f_send.at[q]))
        else:
            wait(fr.at[k, z2, D, lo], f_recv.at[q, 2])
            wait(fr.at[k, z2, D, hi], f_recv.at[q, 3])
            push(fr.at[k, z2, D, rows], fr.at[k, z2, D, rows], f_send.at[q], f_recv.at[q, 4], d_pair)
            finish(lambda: wait(units(7), f_send.at[q]))

    def f4(q):
        k, pair_first, rows, _, _ = split(q)
        if not pair_first:
            wait(fr.at[k, :, 1 - D, rows], f_recv.at[q, 4])

    def s1(q):
        k, pair_first, rows, _, _ = split(q)
        own = g2.at[k, y, A, c, rows]
        if q == 8 * SUB:
            wait(g2.at[pl.ds(8, 8), y, A, c], a_recv.at[0])
        push(own, own, g_send.at[q], g_recv.at[q, 4], a_pair)
        if not pair_first:
            push(own, own, g_send.at[q], g_recv.at[q, 0], y_up)
            push(own, own, g_send.at[q], g_recv.at[q, 1], y_down)

    def s2(q):
        k, pair_first, rows, lo, hi = split(q)
        if pair_first:
            wait(g2.at[k, y, 1 - A, c, rows], g_recv.at[q, 4])
            own = g2.at[k, y, :, c, rows]
            push(own, own, g_send.at[q], g_recv.at[q, 0], y_up)
            push(own, own, g_send.at[q], g_recv.at[q, 1], y_down)
        else:
            b = g2.at[k, y3, A, c]
            wait(b.at[rows], g_recv.at[q, 0])
            push(b.at[lo], b.at[lo], g_send.at[q], g_recv.at[q, 2], y_up)
            push(b.at[rows], b.at[rows], g_send.at[q], g_recv.at[q, 4], a_pair)
            b = g2.at[k, y1, A, c]
            wait(b.at[rows], g_recv.at[q, 1])
            push(b.at[hi], b.at[hi], g_send.at[q], g_recv.at[q, 3], y_down)
            push(b.at[rows], b.at[rows], g_send.at[q], g_recv.at[q, 4], a_pair)

    def s3(q):
        k, pair_first, rows, lo, hi = split(q)
        if pair_first:
            b = g2.at[k, y3, 0, c, rows]
            wait(g2.at[k, y3, :, c, rows], g_recv.at[q, 0])
            push(b, b, g_send.at[q], g_recv.at[q, 2], y_up)
            b = g2.at[k, y1, 1, c, rows]
            wait(g2.at[k, y1, :, c, rows], g_recv.at[q, 1])
            push(b, b, g_send.at[q], g_recv.at[q, 3], y_down)
        else:
            b = g2.at[k, y2, A, c]
            wait(b.at[lo], g_recv.at[q, 2])
            wait(b.at[hi], g_recv.at[q, 3])
            push(b.at[rows], b.at[rows], g_send.at[q], g_recv.at[q, 4], a_pair)

    def s4(q):
        k, pair_first, rows, lo, hi = split(q)
        if pair_first:
            wait(g2.at[k, y2, 0, c, rows], g_recv.at[q, 2])
            wait(g2.at[k, y2, 1, c, rows], g_recv.at[q, 3])
        else:
            wait(g2.at[k, :, 1 - A, c, rows], g_recv.at[q, 4])
        mine = g2.at[k, :, :, c, rows]
        push(mine, mine, g_send.at[q], g_recv.at[q, 5], sibling)
        finish(lambda: wait(units(15), g_send.at[q]))

    def s5(q):
        k, _, rows, _, _ = split(q)
        wait(g2.at[k, :, :, 1 - c, rows], g_recv.at[q, 5])

    def halfway(i):
        for q in range(2):
            acc = jnp.zeros((512, 256), F32)
            for m in range(8):
                rows = fr[pl.ds(4 * q, 4), m // 2, m % 2].reshape(512, 256)
                acc += jnp.dot(rows, g2[8 + i, m // 2, m % 2].reshape(256, 256), preferred_element_type=F32)
            half[pl.ds(4 * q, 4), pl.ds((i % 2) * 128, 128)] = acc.astype(BF16).reshape(4, 128, 256)

    def ladder(j, q):
        acc = jnp.zeros((256, 1024), F32)
        for p in range(8):
            acc += lax.dot_general(half[p], g2[p, pl.ds(2 * q, 2)].reshape(1024, 256), TRANSPOSED, preferred_element_type=F32)
        for h in range(2):
            for m in range(4):
                block = acc[h * 128:(h + 1) * 128, m * 256:(m + 1) * 256]
                part32[2 * j + h, 2 * q + m // 2, m % 2] = block
                part[2 * j + h, 2 * q + m // 2, m % 2] = block.astype(BF16)

    add = lambda *terms: functools.reduce(lambda a, b: a + b, [t.astype(F32) for t in terms])

    def owner_push(q, src_of, dst, sem):
        for cc in range(2):
            here = jnp.logical_and(on_home_chip, c == cc)
            src = src_of(cc)
            push_or_copy(here, src, dst, q_send.at[q, cc], sem, dev(y, 2 * A + c, z, cc))
            finish(lambda src=src, cc=cc, here=here: pl.when(jnp.logical_not(here))(lambda: wait(src, q_send.at[q, cc])))

    def scatter_first(i, q, block, first, second, two):
        send, rin = o_send.at[q], ring_in.at[i]
        push(block(z2, 0, first), rin.at[0, first], send, o_recv.at[q, 0], z_up)
        push(block(z2, 1, second), rin.at[two, second], send, o_recv.at[q, 1], z_down)
        push(block(z3, 0, first), rin.at[1, first], send, o_recv.at[q, 2], z_down)
        push(block(z1, 1, second), rin.at[two + 1, second], send, o_recv.at[q, 3], z_up)

    def o1(q):
        i, ring_first, rows, lo, hi = split(q)
        if ring_first:
            scatter_first(i, q, lambda zz, d, r: part.at[i, zz, d, r], rows, rows, 3)
        else:
            owner_push(q, lambda cc: part.at[i, :, cc, rows], pin.at[i, D, :, rows], o_recv.at[q, 4])

    def o2(q):
        i, ring_first, rows, lo, hi = split(q)
        rin = ring_in.at[i]
        if ring_first:
            wait(rin.at[0, rows], o_recv.at[q, 0])
            comb[i, 0, rows] = add(part32[i, z1, 0, rows], ring_in[i, 0, rows]).astype(BF16)
            push(comb.at[i, 0, rows], rin.at[2, rows], o_send.at[q], o_recv.at[q, 2], z_up)
            wait(rin.at[3, rows], o_recv.at[q, 1])
            comb[i, 1, rows] = add(part32[i, z3, 1, rows], ring_in[i, 3, rows]).astype(BF16)
            push(comb.at[i, 1, rows], rin.at[5, rows], o_send.at[q], o_recv.at[q, 3], z_down)
        else:
            wait(pin.at[i, :, :, rows], o_recv.at[q, 4])
            pp[i, :, rows] = add(pin[i, 0, :, rows], pin[i, 1, :, rows]).astype(BF16)
            scatter_first(i, q, lambda zz, d, r: pp.at[i, zz, r], lo, hi, 0)

    def o3(q):
        i, ring_first, rows, lo, hi = split(q)
        rin = ring_in.at[i]
        if ring_first:
            wait(rin.at[pl.ds(1, 2), rows], o_recv.at[q, 2])
            wait(rin.at[pl.ds(4, 2), rows], o_recv.at[q, 3])
            quad[i, 0, rows] = add(part32[i, z, 0, rows], ring_in[i, 1, rows], ring_in[i, 2, rows]).astype(BF16)
            quad[i, 1, rows] = add(part32[i, z, 1, rows], ring_in[i, 4, rows], ring_in[i, 5, rows]).astype(BF16)
            owner_push(q, lambda cc: quad.at[i, cc, rows], fin.at[i, D, rows], o_recv.at[q, 4])
            finish(lambda: wait(units(6), o_send.at[q]))
        else:
            wait(rin.at[0, lo], o_recv.at[q, 0])
            comb[i, 0, lo] = add(pin[i, 0, z1, lo], pin[i, 1, z1, lo], ring_in[i, 0, lo]).astype(BF16)
            push(comb.at[i, 0, lo], rin.at[2, lo], o_send.at[q], o_recv.at[q, 2], z_up)
            wait(rin.at[0, hi], o_recv.at[q, 1])
            comb[i, 0, hi] = add(pin[i, 0, z3, hi], pin[i, 1, z3, hi], ring_in[i, 0, hi]).astype(BF16)
            push(comb.at[i, 0, hi], rin.at[2, hi], o_send.at[q], o_recv.at[q, 3], z_down)
            finish(lambda: wait(units(3), o_send.at[q]))

    def o4(q):
        i, ring_first, rows, lo, hi = split(q)
        if ring_first:
            wait(fin.at[i, :, rows], o_recv.at[q, 4])
            out_ref[i, rows] = add(fin[i, 0, rows], fin[i, 1, rows])
        else:
            rin = ring_in.at[i]
            wait(rin.at[pl.ds(1, 2), lo], o_recv.at[q, 2])
            wait(rin.at[pl.ds(1, 2), hi], o_recv.at[q, 3])
            out_ref[i, rows] = add(pin[i, 0, z, rows], pin[i, 1, z, rows], ring_in[i, 1, rows], ring_in[i, 2, rows])

    at(SHARE_AT, -1, share_amplitudes)
    for q in range(8 * SUB):
        at(q - AHEAD, -1, e1, q)
        for s, step in enumerate((f1, f2, f3, f4)):
            at(q + s * FACTOR_LAG, s, step, q)
    for q in range(16 * SUB):
        lag = FACTOR_LAG if q < 8 * SUB else AMP_LAG
        for s, step in enumerate((s1, s2, s3, s4)):
            at(q + s * lag, 4 + s, step, q)
        at(q + 3 * lag + CORE_LAG, 8, s5, q)
    for j in range(4):
        ready = (8 + 2 * j) * SUB + 3 * AMP_LAG + CORE_LAG + READY
        at(ready + 1 * SUB - 1, 10, halfway, 2 * j)
        at(ready + 2 * SUB - 1, 10, halfway, 2 * j + 1)
        at(ready + 2 * SUB, 10, ladder, j, 0)
        at(ready + 2 * SUB + 1, 10, ladder, j, 1)
        for q in range(2 * j * SUB, 2 * (j + 1) * SUB):
            for s, step in enumerate((o1, o2, o3, o4)):
                at(ready + 2 * SUB + 1 + OUT_LAG * s, 11 + s, step, q)
    while plan:
        now[0], _, _, step, args = heapq.heappop(plan)
        step(*args)


def shards(amplitudes, df_factor, amp_mask, factor_mask):
    vmem, smem = pl.BlockSpec(memory_space=pltpu.VMEM), pl.BlockSpec(memory_space=pltpu.SMEM)
    block = lambda *lead: pltpu.VMEM((*lead, 128, 256), BF16)
    dma = lambda *shape: pltpu.SemaphoreType.DMA(shape)
    return pl.pallas_call(
        kernel,
        out_shape=jax.ShapeDtypeStruct((8, 128, 256), F32),
        in_specs=[vmem, vmem, smem, smem],
        out_specs=vmem,
        scratch_shapes=[
            pltpu.VMEM((8, 16, 2048), BF16),
            block(8),
            block(16, 4, 2, 2),
            block(8, 4, 2),
            pltpu.VMEM((8, 256, 256), BF16),
            block(8, 4, 2),
            pltpu.VMEM((8, 4, 2, 128, 256), F32),
            block(8, 6),
            block(8, 2),
            block(8, 2),
            block(8, 2),
            block(8, 2, 4),
            block(8, 4),
            dma(16 * SUB, 6), dma(16 * SUB), dma(8 * SUB, 6), dma(8 * SUB), dma(8 * SUB, 2), dma(1), dma(4, 2),
            dma(8 * SUB, 5), dma(8 * SUB), dma(8 * SUB, 2),
        ],
        compiler_params=pltpu.CompilerParams(collective_id=0, has_side_effects=True, vmem_limit_bytes=60 * 2**20),
        cost_estimate=pl.CostEstimate(flops=17179869184, bytes_accessed=4 * 2**20, transcendentals=0),
    )(amplitudes, df_factor, amp_mask, factor_mask)


def solution(mesh):
    return jax.shard_map(
        shards,
        mesh=mesh,
        in_specs=(P(None, ("wide", "narrow"), None), P(None, "wide", "narrow"), P(), P()),
        out_specs=P(None, "wide", "narrow"),
        check_vma=False,
    )
```

```python
import functools
import heapq

import jax
import jax.numpy as jnp
from jax import lax
from jax.experimental import pallas as pl
from jax.experimental.pallas import tpu as pltpu
from jax.sharding import PartitionSpec as P

MESH = pl.DeviceIdType.MESH
BF16 = jnp.bfloat16
F32 = jnp.float32
TRANSPOSED = (((1,), (1,)), ((), ()))

SUB = 2
ROWS = 128 // SUB
FACTOR_LAG = 3.0
AMP_LAG = 3.0
CORE_LAG = 1.0
OUT_LAG = 4.0
AHEAD = 6
SHARE_AT = 0.0
END_LAG = 8.0
RING_FIRST = (1, 3, 5, 7)
ROW_RING_FIRST = (1, 4, 6)
ROW_STEP = 2.25
ROW_LAG = 3.5
SECOND_HOP = 10.0
ORDER = (0, 1, 2, 3, 4, 5, 6, 7, 8, 9, 10, 11, 12, 13, 14, 15)
GROUPS = ((0, 1), (2, 3), (4, 5), (6,), (7,))


def kernel(amp_ref, fac_ref, amask, fmask, out_ref, tsrc, tmid, fsrc, g2, fr, half, part, part32, ring_in, comb, quad, fin, pin, pp,
           g_recv, g_send, core_recv, f_recv, f_all, f_send, e_send, a_recv, a_send, o_recv, o_send, q_send):
    w, n = lax.axis_index("wide"), lax.axis_index("narrow")
    y, x = w // 4, w % 4
    z, c = n // 2, n % 2
    A, xl = x // 2, x % 2
    D = ((x + 1) // 2) % 2
    up = lambda v, s: lax.rem(v + s + 4, 4)
    x_of = lambda a, d: a * 3 + d * (1 - 2 * a)
    dev = lambda yy, xx, zz, cc: (yy * 4 + xx, zz * 2 + cc)
    z1, z2, z3 = up(z, 1), up(z, 2), up(z, 3)
    y1, y2, y3 = up(y, 1), up(y, 2), up(y, 3)
    z_up, z_down = dev(y, x, z1, c), dev(y, x, z3, c)
    y_up, y_down = dev(y1, x, z, c), dev(y3, x, z, c)
    a_pair = dev(y, x_of(1 - A, D), z, c)
    d_pair = dev(y, x_of(A, 1 - D), z, c)
    sibling = dev(y, x, z, 1 - c)
    on_home_chip = x == 2 * A + c

    def push(src, dst, send, recv, to):
        pltpu.make_async_remote_copy(src_ref=src, dst_ref=dst, send_sem=send, recv_sem=recv, device_id=to, device_id_type=MESH).start()

    def push_or_copy(here, src, dst, send, recv, to):
        @pl.when(here)
        def _():
            pltpu.make_async_copy(src, dst, recv).start()

        @pl.when(jnp.logical_not(here))
        def _():
            push(src, dst, send, recv, to)

    def wait(ref, sem):
        pltpu.make_async_copy(ref, ref, sem).wait()

    def units(count, rows=ROWS):
        sizes = [(a, b, d, e) for a in range(1, 17) for b in range(1, 5) for d in (1, 2) for e in (1, 2) if a * b * d * e == count]
        a, b, d, e = sizes[0]
        return g2.at[pl.ds(0, a), pl.ds(0, b), pl.ds(0, d), pl.ds(0, e), pl.ds(0, rows)]

    def split(k, h, tall):
        first = h * tall
        pair_first = (k % 8 not in RING_FIRST) if tall == 128 else (h == 0 or k % 8 == 7)
        return pair_first, pl.ds(first, tall), pl.ds(first, tall // 2), pl.ds(first + tall // 2, tall // 2)

    barrier = pltpu.get_barrier_semaphore()
    for to in (sibling, d_pair, dev(y, x_of(A, 1 - D), z, 1 - c), z_up, z_down, dev(y, x, z2, c), y_up, y_down, a_pair):
        pl.semaphore_signal(barrier, inc=1, device_id=to, device_id_type=MESH)

    for h in range(2):
        keep = fmask[w, 2 * n + h].astype(F32)
        cols = pl.ds(h * 128, 128)
        fsrc[:, :, cols] = (fac_ref[:, :, cols].astype(F32) * keep).astype(BF16)
    for h in range(16):
        keep = amask[w, h].astype(F32)
        cols = pl.ds(h * 128, 128)
        tsrc[h // 4, (h // 2) % 2, :, :, pl.ds((h % 2) * 128, 128)] = (amp_ref[:, :, cols].astype(F32) * keep).astype(BF16)

    pl.semaphore_wait(barrier, 9)

    plan = []
    now = [-100.0, 0]

    def at(when, order, step, *args):
        now[1] += 1
        heapq.heappush(plan, (when, order, now[1], step, args))

    def finish(step):
        at(now[0] + END_LAG, 30, step)

    stays = [jnp.logical_and(x_of(A, d) == x, xl == c) for d in range(2)]

    def e1(k):
        for d in range(2):
            def go(d=d):
                push_or_copy(stays[d], fsrc.at[k], fr.at[k, z, c], e_send.at[d], f_recv.at[k, 0], dev(y, x_of(A, d), z, xl))

            if k in ROW_RING_FIRST:
                pl.when(c == d)(go)
            else:
                go()

    def e_end():
        for d in range(2):
            goes = jnp.logical_not(stays[d])
            pl.when(jnp.logical_and(goes, c == d))(lambda: wait(fsrc, e_send.at[d]))
            pl.when(jnp.logical_and(goes, c != d))(lambda: wait(fsrc.at[pl.ds(0, 8 - len(ROW_RING_FIRST))], e_send.at[d]))

    def t1():
        for d in range(2):
            dst = tmid.at[:, :, pl.ds(pl.multiple_of(c * 16, 16), 16)]
            push_or_copy(stays[d], tsrc.at[:, d], dst, a_send.at[d], a_recv.at[0], dev(y, x_of(A, d), z, xl))
            finish(lambda d=d: pl.when(jnp.logical_not(stays[d]))(lambda: wait(tsrc.at[:, d], a_send.at[d])))

    def t2():
        wait(tmid, a_recv.at[0])
        dst = g2.at[pl.ds(8, 8), y, A, c, pl.ds(pl.multiple_of(z * 32, 32), 32)]
        for zz in (z2, z1, z3):
            push(tmid.at[zz], dst, a_send.at[2], a_recv.at[1], dev(y, x, zz, c))
        pltpu.make_async_copy(tmid.at[z], dst, a_recv.at[1]).start()
        finish(lambda: wait(tmid.at[pl.ds(0, 3)], a_send.at[2]))

    def t3():
        wait(g2.at[pl.ds(8, 8), y, A, c], a_recv.at[1])

    def f0(k):
        wait(fr.at[k, z] if k not in ROW_RING_FIRST else fr.at[k, z, D], f_recv.at[k, 0])
        g2[k, y, A, c] = fr[k, z, D]

    def f1(k):
        pair_first = k not in ROW_RING_FIRST
        own = fr.at[k, z] if pair_first else fr.at[k, z, D]
        push(own, own, f_send.at[k], f_recv.at[k, 1], z_up)
        push(own, own, f_send.at[k], f_recv.at[k, 1], z_down)
        if not pair_first:
            push(own, own, f_send.at[k], f_all.at[0], d_pair)

    def f2(k):
        pair_first, lo, hi = k not in ROW_RING_FIRST, pl.ds(0, 64), pl.ds(64, 64)
        wait(units(4 if pair_first else 2, 128), f_recv.at[k, 1])
        if pair_first:
            push(fr.at[k, z3, 0], fr.at[k, z3, 0], f_send.at[k], f_all.at[0], z_up)
            push(fr.at[k, z1, 1], fr.at[k, z1, 1], f_send.at[k], f_all.at[0], z_down)
        else:
            push(fr.at[k, z3, D, lo], fr.at[k, z3, D, lo], f_send.at[k], f_recv.at[k, 2], z_up)
            push(fr.at[k, z1, D, hi], fr.at[k, z1, D, hi], f_send.at[k], f_recv.at[k, 2], z_down)
            push(fr.at[k, z3, D], fr.at[k, z3, D], f_send.at[k], f_all.at[0], d_pair)
            push(fr.at[k, z1, D], fr.at[k, z1, D], f_send.at[k], f_all.at[0], d_pair)

    def f3(k):
        pair_first, lo, hi = k not in ROW_RING_FIRST, pl.ds(0, 64), pl.ds(64, 64)
        if not pair_first:
            wait(fr.at[k, z2, D], f_recv.at[k, 2])
            push(fr.at[k, z2, D], fr.at[k, z2, D], f_send.at[k], f_all.at[0], d_pair)
        finish(lambda: wait(units(6 if pair_first else 7, 128), f_send.at[k]))

    def f4():
        wait(units(2 * (8 - len(ROW_RING_FIRST)) + 4 * len(ROW_RING_FIRST), 128), f_all.at[0])

    def s1(k, h, tall, at_sem):
        pair_first, rows, _, _ = split(k, h, tall)
        own = g2.at[k, y, A, c, rows]
        push(own, own, g_send.at[at_sem], g_recv.at[at_sem, 2], a_pair)
        if not pair_first:
            push(own, own, g_send.at[at_sem], g_recv.at[at_sem, 0], y_up)
            push(own, own, g_send.at[at_sem], g_recv.at[at_sem, 0], y_down)

    def s2(k, h, tall, at_sem):
        pair_first, rows, lo, hi = split(k, h, tall)
        send, recv = g_send.at[at_sem], g_recv.at[at_sem]
        if pair_first:
            wait(g2.at[k, y, 1 - A, c, rows], recv.at[2])
            own = g2.at[k, y, :, c, rows]
            push(own, own, send, recv.at[0], y_up)
            push(own, own, send, recv.at[0], y_down)
        else:
            wait(units(2, tall), recv.at[0])
            b, d = g2.at[k, y3, A, c], g2.at[k, y1, A, c]
            push(b.at[lo], b.at[lo], send, recv.at[1], y_up)
            push(d.at[hi], d.at[hi], send, recv.at[1], y_down)
            push(b.at[rows], b.at[rows], send, recv.at[2], a_pair)
            push(d.at[rows], d.at[rows], send, recv.at[2], a_pair)

    def s3(k, h, tall, at_sem):
        pair_first, rows, lo, hi = split(k, h, tall)
        send, recv = g_send.at[at_sem], g_recv.at[at_sem]
        if pair_first:
            wait(units(4, tall), recv.at[0])
            b, d = g2.at[k, y3, 0, c, rows], g2.at[k, y1, 1, c, rows]
            push(b, b, send, recv.at[1], y_up)
            push(d, d, send, recv.at[1], y_down)
        else:
            b = g2.at[k, y2, A, c, rows]
            wait(b, recv.at[1])
            push(b, b, send, recv.at[2], a_pair)

    def s4(k, h, tall, at_sem):
        pair_first, rows, lo, hi = split(k, h, tall)
        if pair_first:
            wait(g2.at[k, y2, :, c, rows], g_recv.at[at_sem, 1])
        else:
            wait(g2.at[k, :, 1 - A, c, rows], g_recv.at[at_sem, 2])
        mine = g2.at[k, :, :, c, rows]
        push(mine, mine, g_send.at[at_sem], core_recv.at[0 if k < 8 else k - 7], sibling)
        finish(lambda: wait(units(15, tall), g_send.at[at_sem]))

    def columns_in():
        wait(g2.at[pl.ds(0, 8), :, :, 1 - c], core_recv.at[0])

    def amps_in(k):
        wait(g2.at[k, :, :, 1 - c], core_recv.at[k - 7])

    def halfway(i, slot):
        for q in range(2):
            acc = jnp.zeros((512, 256), F32)
            for m in range(8):
                rows = fr[pl.ds(4 * q, 4), m // 2, m % 2].reshape(512, 256)
                acc += jnp.dot(rows, g2[8 + i, m // 2, m % 2].reshape(256, 256), preferred_element_type=F32)
            half[pl.ds(4 * q, 4), pl.ds(slot * 128, 128)] = acc.astype(BF16).reshape(4, 128, 256)

    def ladder(group, q):
        tall = pl.ds(0, 128 * len(group))
        acc = jnp.zeros((128 * len(group), 1024), F32)
        for p in range(8):
            acc += lax.dot_general(half[p, tall], g2[p, pl.ds(2 * q, 2)].reshape(1024, 256), TRANSPOSED, preferred_element_type=F32)
        for h, i in enumerate(group):
            for m in range(4):
                block = acc[h * 128:(h + 1) * 128, m * 256:(m + 1) * 256]
                part32[i, 2 * q + m // 2, m % 2] = block
                part[i, 2 * q + m // 2, m % 2] = block.astype(BF16)

    add = lambda *terms: functools.reduce(lambda a, b: a + b, [t.astype(F32) for t in terms])

    owns = [jnp.logical_and(on_home_chip, c == cc) for cc in range(2)]

    def owner_push(src_of, dst, send, sem):
        for cc in range(2):
            push_or_copy(owns[cc], src_of(cc), dst, q_send.at[send, cc], sem, dev(y, 2 * A + c, z, cc))

    def q_end():
        for cc in range(2):
            for send, count in enumerate(sent):
                pl.when(jnp.logical_not(owns[cc]))(lambda: wait(units(count), q_send.at[send, cc]))

    sent = [0, 0]

    def scatter_first(i, q, block, first, second, two):
        send, rin = o_send.at[q], ring_in.at[i]
        push(block(z2, 0, first), rin.at[0, first], send, o_recv.at[q, 0], z_up)
        push(block(z2, 1, second), rin.at[two, second], send, o_recv.at[q, 0], z_down)
        push(block(z3, 0, first), rin.at[1, first], send, o_recv.at[q, 1], z_down)
        push(block(z1, 1, second), rin.at[two + 1, second], send, o_recv.at[q, 1], z_up)

    def o1(i, h):
        ring_first, rows, lo, hi = split(i, h, ROWS)
        q = i * SUB + h
        if ring_first:
            scatter_first(i, q, lambda zz, d, r: part.at[i, zz, d, r], rows, rows, 3)
        else:
            owner_push(lambda cc: part.at[i, :, cc, rows], pin.at[i, D, :, rows], 1, o_recv.at[q, 2])
            sent[1] += 4

    def o2(i, h):
        ring_first, rows, lo, hi = split(i, h, ROWS)
        q = i * SUB + h
        rin = ring_in.at[i]
        if ring_first:
            wait(units(2), o_recv.at[q, 0])
            comb[i, 0, rows] = add(part32[i, z1, 0, rows], ring_in[i, 0, rows]).astype(BF16)
            push(comb.at[i, 0, rows], rin.at[2, rows], o_send.at[q], o_recv.at[q, 1], z_up)
            comb[i, 1, rows] = add(part32[i, z3, 1, rows], ring_in[i, 3, rows]).astype(BF16)
            push(comb.at[i, 1, rows], rin.at[5, rows], o_send.at[q], o_recv.at[q, 1], z_down)
        else:
            wait(pin.at[i, :, :, rows], o_recv.at[q, 2])
            pp[i, :, rows] = add(pin[i, 0, :, rows], pin[i, 1, :, rows]).astype(BF16)
            scatter_first(i, q, lambda zz, d, r: pp.at[i, zz, r], lo, hi, 0)

    def o3(i, h):
        ring_first, rows, lo, hi = split(i, h, ROWS)
        q = i * SUB + h
        rin = ring_in.at[i]
        if ring_first:
            wait(units(4), o_recv.at[q, 1])
            quad[i, 0, rows] = add(part32[i, z, 0, rows], ring_in[i, 1, rows], ring_in[i, 2, rows]).astype(BF16)
            quad[i, 1, rows] = add(part32[i, z, 1, rows], ring_in[i, 4, rows], ring_in[i, 5, rows]).astype(BF16)
            owner_push(lambda cc: quad.at[i, cc, rows], fin.at[i, D, rows], 0, o_recv.at[q, 2])
            sent[0] += 1
            finish(lambda: wait(units(6), o_send.at[q]))
        else:
            wait(rin.at[0, rows], o_recv.at[q, 0])
            comb[i, 0, lo] = add(pin[i, 0, z1, lo], pin[i, 1, z1, lo], ring_in[i, 0, lo]).astype(BF16)
            push(comb.at[i, 0, lo], rin.at[2, lo], o_send.at[q], o_recv.at[q, 1], z_up)
            comb[i, 0, hi] = add(pin[i, 0, z3, hi], pin[i, 1, z3, hi], ring_in[i, 0, hi]).astype(BF16)
            push(comb.at[i, 0, hi], rin.at[2, hi], o_send.at[q], o_recv.at[q, 1], z_down)
            finish(lambda: wait(units(3), o_send.at[q]))

    def o4(i, h):
        ring_first, rows, lo, hi = split(i, h, ROWS)
        q = i * SUB + h
        if ring_first:
            wait(fin.at[i, :, rows], o_recv.at[q, 2])
            out_ref[i, rows] = add(fin[i, 0, rows], fin[i, 1, rows])
        else:
            wait(units(2), o_recv.at[q, 1])
            out_ref[i, rows] = add(pin[i, 0, z, rows], pin[i, 1, z, rows], ring_in[i, 1, rows], ring_in[i, 2, rows])

    at(SHARE_AT, -1, t1)
    at(SECOND_HOP, -1, t2)
    for k in range(8):
        at(k * SUB - AHEAD, -2, e1, k)
        at(k * SUB, -1, f0, k)
        for s, step in enumerate((f1, f2, f3)):
            at(k * ROW_STEP + s * ROW_LAG, s, step, k)
    rows_done = 7 * ROW_STEP + 2 * ROW_LAG + 2
    at(rows_done, 9, f4)
    at(8 * SUB, 31, e_end)
    done = {}
    amps_at = None
    for place, k in enumerate(ORDER):
        lag, parts = (FACTOR_LAG, 1) if k < 8 else (AMP_LAG, SUB)
        if k >= 8 and amps_at is None:
            amps_at = place * SUB
            at(amps_at, 3, t3)
        for h in range(parts):
            start = place * SUB + h
            for s, step in enumerate((s1, s2, s3, s4)):
                at(start + s * lag, 4 + s, step, k, h, 128 // parts, k if k < 8 else 8 + (k - 8) * SUB + h)
        done[k] = place * SUB + parts - 1 + 3 * lag + CORE_LAG
        if k >= 8:
            at(done[k], 8, amps_in, k)
    columns_done = max(done[k] for k in range(8))
    at(columns_done, 8, columns_in)
    last = 0
    for group in GROUPS:
        when = max(rows_done, last)
        for slot, i in enumerate(group):
            when = max(when, done[8 + i])
            at(when, 10, halfway, i, slot)
            when += 1
        when = max(when, columns_done)
        at(when, 10, ladder, group, 0)
        last = when + 1
        at(last, 10, ladder, group, 1)
        for i in group:
            for h in range(SUB):
                for s, step in enumerate((o1, o2, o3, o4)):
                    at(last + OUT_LAG * s, 11 + s, step, i, h)
    at(1000, 40, q_end)
    while plan:
        now[0], _, _, step, args = heapq.heappop(plan)
        step(*args)


def shards(amplitudes, df_factor, amp_mask, factor_mask):
    vmem, smem = pl.BlockSpec(memory_space=pltpu.VMEM), pl.BlockSpec(memory_space=pltpu.SMEM)
    block = lambda *lead: pltpu.VMEM((*lead, 128, 256), BF16)
    dma = lambda *shape: pltpu.SemaphoreType.DMA(shape)
    return pl.pallas_call(
        kernel,
        out_shape=jax.ShapeDtypeStruct((8, 128, 256), F32),
        in_specs=[vmem, vmem, smem, smem],
        out_specs=vmem,
        scratch_shapes=[
            pltpu.VMEM((4, 2, 8, 16, 256), BF16),
            pltpu.VMEM((4, 8, 32, 256), BF16),
            block(8),
            block(16, 4, 2, 2),
            block(8, 4, 2),
            pltpu.VMEM((8, 256, 256), BF16),
            block(8, 4, 2),
            pltpu.VMEM((8, 4, 2, 128, 256), F32),
            block(8, 6),
            block(8, 2),
            block(8, 2),
            block(8, 2),
            block(8, 2, 4),
            block(8, 4),
            dma(8 + 8 * SUB, 3), dma(8 + 8 * SUB), dma(9), dma(8, 3), dma(1), dma(8), dma(2), dma(2), dma(3),
            dma(8 * SUB, 3), dma(8 * SUB), dma(2, 2),
        ],
        compiler_params=pltpu.CompilerParams(collective_id=0, has_side_effects=True, vmem_limit_bytes=60 * 2**20),
        cost_estimate=pl.CostEstimate(flops=17179869184, bytes_accessed=4 * 2**20, transcendentals=0),
    )(amplitudes, df_factor, amp_mask, factor_mask)


def solution(mesh):
    return jax.shard_map(
        shards,
        mesh=mesh,
        in_specs=(P(None, ("wide", "narrow"), None), P(None, "wide", "narrow"), P(), P()),
        out_specs=P(None, "wide", "narrow"),
        check_vma=False,
    )
```

```python
import functools
import heapq

import jax
import jax.numpy as jnp
from jax import lax
from jax.experimental import pallas as pl
from jax.experimental.pallas import tpu as pltpu
from jax.sharding import PartitionSpec as P

MESH = pl.DeviceIdType.MESH
BF16 = jnp.bfloat16
F32 = jnp.float32
TRANSPOSED = (((1,), (1,)), ((), ()))

SUB = 2
ROWS = 128 // SUB
FACTOR_LAG = 3.0
AMP_LAG = 3.0
CORE_LAG = 1.0
OUT_LAG = 4.0
AHEAD = 6
SHARE_AT = 0.0
END_LAG = 8.0
RING_FIRST = (1, 3, 5, 7)
ROW_RING_FIRST = (1, 4, 6)
ROW_STEP = 2.25
ROW_LAG = 5.0
SECOND_HOP = 10.0
ORDER = (0, 1, 2, 3, 4, 5, 6, 7, 8, 9, 10, 11, 12, 13, 14, 15)
GROUPS = ((0, 1), (2, 3), (4, 5), (6, 7))


def kernel(amp_ref, fac_ref, amask, fmask, out_ref, tsrc, tmid, fsrc, g2, fr, half, part, part32, ring_in, comb, quad, fin, pin, pp,
           g_recv, g_send, core_recv, f_recv, f_all, f_send, e_send, a_recv, a_send, o_recv, o_send, q_send):
    w, n = lax.axis_index("wide"), lax.axis_index("narrow")
    y, x = w // 4, w % 4
    z, c = n // 2, n % 2
    A, xl = x // 2, x % 2
    D = ((x + 1) // 2) % 2
    up = lambda v, s: lax.rem(v + s + 4, 4)
    x_of = lambda a, d: a * 3 + d * (1 - 2 * a)
    dev = lambda yy, xx, zz, cc: (yy * 4 + xx, zz * 2 + cc)
    z1, z2, z3 = up(z, 1), up(z, 2), up(z, 3)
    y1, y2, y3 = up(y, 1), up(y, 2), up(y, 3)
    z_up, z_down = dev(y, x, z1, c), dev(y, x, z3, c)
    y_up, y_down = dev(y1, x, z, c), dev(y3, x, z, c)
    a_pair = dev(y, x_of(1 - A, D), z, c)
    d_pair = dev(y, x_of(A, 1 - D), z, c)
    sibling = dev(y, x, z, 1 - c)
    on_home_chip = x == 2 * A + c

    def push(src, dst, send, recv, to):
        pltpu.make_async_remote_copy(src_ref=src, dst_ref=dst, send_sem=send, recv_sem=recv, device_id=to, device_id_type=MESH).start()

    def push_or_copy(here, src, dst, send, recv, to):
        @pl.when(here)
        def _():
            pltpu.make_async_copy(src, dst, recv).start()

        @pl.when(jnp.logical_not(here))
        def _():
            push(src, dst, send, recv, to)

    def wait(ref, sem):
        pltpu.make_async_copy(ref, ref, sem).wait()

    def units(count, rows=ROWS):
        sizes = [(a, b, d, e) for a in range(1, 17) for b in range(1, 5) for d in (1, 2) for e in (1, 2) if a * b * d * e == count]
        a, b, d, e = sizes[0]
        return g2.at[pl.ds(0, a), pl.ds(0, b), pl.ds(0, d), pl.ds(0, e), pl.ds(0, rows)]

    def split(k, h, tall):
        first = h * tall
        pair_first = (k % 8 not in RING_FIRST) if tall == 128 else (h == 0 or k % 8 == 7)
        return pair_first, pl.ds(first, tall), pl.ds(first, tall // 2), pl.ds(first + tall // 2, tall // 2)

    barrier = pltpu.get_barrier_semaphore()
    for to in (sibling, d_pair, dev(y, x_of(A, 1 - D), z, 1 - c), z_up, z_down, dev(y, x, z2, c), y_up, y_down, a_pair):
        pl.semaphore_signal(barrier, inc=1, device_id=to, device_id_type=MESH)

    for h in range(2):
        keep = fmask[w, 2 * n + h].astype(F32)
        cols = pl.ds(h * 128, 128)
        fsrc[:, :, cols] = (fac_ref[:, :, cols].astype(F32) * keep).astype(BF16)
    for h in range(16):
        keep = amask[w, h].astype(F32)
        cols = pl.ds(h * 128, 128)
        tsrc[h // 4, (h // 2) % 2, :, :, pl.ds((h % 2) * 128, 128)] = (amp_ref[:, :, cols].astype(F32) * keep).astype(BF16)

    pl.semaphore_wait(barrier, 9)

    plan = []
    now = [-100.0, 0]

    def at(when, order, step, *args):
        now[1] += 1
        heapq.heappush(plan, (when, order, now[1], step, args))

    def finish(step):
        at(now[0] + END_LAG, 30, step)

    stays = [jnp.logical_and(x_of(A, d) == x, xl == c) for d in range(2)]

    def e1(k):
        for d in range(2):
            def go(d=d):
                push_or_copy(stays[d], fsrc.at[k], fr.at[k, z, c], e_send.at[d], f_recv.at[k, 0], dev(y, x_of(A, d), z, xl))

            if k in ROW_RING_FIRST:
                pl.when(c == d)(go)
            else:
                go()

    def e_end():
        for d in range(2):
            goes = jnp.logical_not(stays[d])
            pl.when(jnp.logical_and(goes, c == d))(lambda: wait(fsrc, e_send.at[d]))
            pl.when(jnp.logical_and(goes, c != d))(lambda: wait(fsrc.at[pl.ds(0, 8 - len(ROW_RING_FIRST))], e_send.at[d]))

    def t1():
        for d in range(2):
            dst = tmid.at[:, :, pl.ds(pl.multiple_of(c * 16, 16), 16)]
            push_or_copy(stays[d], tsrc.at[:, d], dst, a_send.at[d], a_recv.at[0], dev(y, x_of(A, d), z, xl))
            finish(lambda d=d: pl.when(jnp.logical_not(stays[d]))(lambda: wait(tsrc.at[:, d], a_send.at[d])))

    def t2():
        wait(tmid, a_recv.at[0])
        dst = g2.at[pl.ds(8, 8), y, A, c, pl.ds(pl.multiple_of(z * 32, 32), 32)]
        for zz in (z2, z1, z3):
            push(tmid.at[zz], dst, a_send.at[2], a_recv.at[1], dev(y, x, zz, c))
        pltpu.make_async_copy(tmid.at[z], dst, a_recv.at[1]).start()
        finish(lambda: wait(tmid.at[pl.ds(0, 3)], a_send.at[2]))

    def t3():
        wait(g2.at[pl.ds(8, 8), y, A, c], a_recv.at[1])

    def f0(k):
        wait(fr.at[k, z] if k not in ROW_RING_FIRST else fr.at[k, z, D], f_recv.at[k, 0])
        g2[k, y, A, c] = fr[k, z, D]

    def f1(k):
        pair_first = k not in ROW_RING_FIRST
        own = fr.at[k, z] if pair_first else fr.at[k, z, D]
        push(own, own, f_send.at[k], f_recv.at[k, 1], z_up)
        push(own, own, f_send.at[k], f_recv.at[k, 1], z_down)
        if not pair_first:
            push(own, own, f_send.at[k], f_all.at[0], d_pair)

    def f2(k):
        pair_first, lo, hi = k not in ROW_RING_FIRST, pl.ds(0, 64), pl.ds(64, 64)
        wait(units(4 if pair_first else 2, 128), f_recv.at[k, 1])
        if pair_first:
            push(fr.at[k, z3, 0], fr.at[k, z3, 0], f_send.at[k], f_all.at[0], z_up)
            push(fr.at[k, z1, 1], fr.at[k, z1, 1], f_send.at[k], f_all.at[0], z_down)
        else:
            push(fr.at[k, z3, D, lo], fr.at[k, z3, D, lo], f_send.at[k], f_recv.at[k, 2], z_up)
            push(fr.at[k, z1, D, hi], fr.at[k, z1, D, hi], f_send.at[k], f_recv.at[k, 2], z_down)
            push(fr.at[k, z3, D], fr.at[k, z3, D], f_send.at[k], f_all.at[0], d_pair)
            push(fr.at[k, z1, D], fr.at[k, z1, D], f_send.at[k], f_all.at[0], d_pair)

    def f3(k):
        pair_first, lo, hi = k not in ROW_RING_FIRST, pl.ds(0, 64), pl.ds(64, 64)
        if not pair_first:
            wait(fr.at[k, z2, D], f_recv.at[k, 2])
            push(fr.at[k, z2, D], fr.at[k, z2, D], f_send.at[k], f_all.at[0], d_pair)
        finish(lambda: wait(units(6 if pair_first else 7, 128), f_send.at[k]))

    def f4():
        wait(units(2 * (8 - len(ROW_RING_FIRST)) + 4 * len(ROW_RING_FIRST), 128), f_all.at[0])

    def s1(k, h, tall, at_sem):
        pair_first, rows, _, _ = split(k, h, tall)
        own = g2.at[k, y, A, c, rows]
        push(own, own, g_send.at[at_sem], g_recv.at[at_sem, 2], a_pair)
        if not pair_first:
            push(own, own, g_send.at[at_sem], g_recv.at[at_sem, 0], y_up)
            push(own, own, g_send.at[at_sem], g_recv.at[at_sem, 0], y_down)

    def s2(k, h, tall, at_sem):
        pair_first, rows, lo, hi = split(k, h, tall)
        send, recv = g_send.at[at_sem], g_recv.at[at_sem]
        if pair_first:
            wait(g2.at[k, y, 1 - A, c, rows], recv.at[2])
            own = g2.at[k, y, :, c, rows]
            push(own, own, send, recv.at[0], y_up)
            push(own, own, send, recv.at[0], y_down)
        else:
            wait(units(2, tall), recv.at[0])
            b, d = g2.at[k, y3, A, c], g2.at[k, y1, A, c]
            push(b.at[lo], b.at[lo], send, recv.at[1], y_up)
            push(d.at[hi], d.at[hi], send, recv.at[1], y_down)
            push(b.at[rows], b.at[rows], send, recv.at[2], a_pair)
            push(d.at[rows], d.at[rows], send, recv.at[2], a_pair)

    def s3(k, h, tall, at_sem):
        pair_first, rows, lo, hi = split(k, h, tall)
        send, recv = g_send.at[at_sem], g_recv.at[at_sem]
        if pair_first:
            wait(units(4, tall), recv.at[0])
            b, d = g2.at[k, y3, 0, c, rows], g2.at[k, y1, 1, c, rows]
            push(b, b, send, recv.at[1], y_up)
            push(d, d, send, recv.at[1], y_down)
        else:
            b = g2.at[k, y2, A, c, rows]
            wait(b, recv.at[1])
            push(b, b, send, recv.at[2], a_pair)

    def s4(k, h, tall, at_sem):
        pair_first, rows, lo, hi = split(k, h, tall)
        if pair_first:
            wait(g2.at[k, y2, :, c, rows], g_recv.at[at_sem, 1])
        else:
            wait(g2.at[k, :, 1 - A, c, rows], g_recv.at[at_sem, 2])
        mine = g2.at[k, :, :, c, rows]
        push(mine, mine, g_send.at[at_sem], core_recv.at[0 if k < 8 else k - 7], sibling)
        finish(lambda: wait(units(15, tall), g_send.at[at_sem]))

    def columns_in():
        wait(g2.at[pl.ds(0, 8), :, :, 1 - c], core_recv.at[0])

    def amps_in(k):
        wait(g2.at[k, :, :, 1 - c], core_recv.at[k - 7])

    def halfway(i, slot):
        for q in range(2):
            acc = jnp.zeros((512, 256), F32)
            for m in range(8):
                rows = fr[pl.ds(4 * q, 4), m // 2, m % 2].reshape(512, 256)
                acc += jnp.dot(rows, g2[8 + i, m // 2, m % 2].reshape(256, 256), preferred_element_type=F32)
            half[pl.ds(4 * q, 4), pl.ds(slot * 128, 128)] = acc.astype(BF16).reshape(4, 128, 256)

    def ladder(group, q):
        tall = pl.ds(0, 128 * len(group))
        acc = jnp.zeros((128 * len(group), 1024), F32)
        for p in range(8):
            acc += lax.dot_general(half[p, tall], g2[p, pl.ds(2 * q, 2)].reshape(1024, 256), TRANSPOSED, preferred_element_type=F32)
        for h, i in enumerate(group):
            for m in range(4):
                block = acc[h * 128:(h + 1) * 128, m * 256:(m + 1) * 256]
                part32[i, 2 * q + m // 2, m % 2] = block
                part[i, 2 * q + m // 2, m % 2] = block.astype(BF16)

    add = lambda *terms: functools.reduce(lambda a, b: a + b, [t.astype(F32) for t in terms])

    owns = [jnp.logical_and(on_home_chip, c == cc) for cc in range(2)]

    def owner_push(src_of, dst, send, sem):
        for cc in range(2):
            push_or_copy(owns[cc], src_of(cc), dst, q_send.at[send, cc], sem, dev(y, 2 * A + c, z, cc))

    def q_end():
        for cc in range(2):
            for send, count in enumerate(sent):
                pl.when(jnp.logical_not(owns[cc]))(lambda: wait(units(count), q_send.at[send, cc]))

    sent = [0, 0]

    def scatter_first(i, q, block, first, second, two):
        send, rin = o_send.at[q], ring_in.at[i]
        push(block(z2, 0, first), rin.at[0, first], send, o_recv.at[q, 0], z_up)
        push(block(z2, 1, second), rin.at[two, second], send, o_recv.at[q, 0], z_down)
        push(block(z3, 0, first), rin.at[1, first], send, o_recv.at[q, 1], z_down)
        push(block(z1, 1, second), rin.at[two + 1, second], send, o_recv.at[q, 1], z_up)

    def o1(i, h):
        ring_first, rows, lo, hi = split(i, h, ROWS)
        q = i * SUB + h
        if ring_first:
            scatter_first(i, q, lambda zz, d, r: part.at[i, zz, d, r], rows, rows, 3)
        else:
            owner_push(lambda cc: part.at[i, :, cc, rows], pin.at[i, D, :, rows], 1, o_recv.at[q, 2])
            sent[1] += 4

    def o2(i, h):
        ring_first, rows, lo, hi = split(i, h, ROWS)
        q = i * SUB + h
        rin = ring_in.at[i]
        if ring_first:
            wait(units(2), o_recv.at[q, 0])
            comb[i, 0, rows] = add(part32[i, z1, 0, rows], ring_in[i, 0, rows]).astype(BF16)
            push(comb.at[i, 0, rows], rin.at[2, rows], o_send.at[q], o_recv.at[q, 1], z_up)
            comb[i, 1, rows] = add(part32[i, z3, 1, rows], ring_in[i, 3, rows]).astype(BF16)
            push(comb.at[i, 1, rows], rin.at[5, rows], o_send.at[q], o_recv.at[q, 1], z_down)
        else:
            wait(pin.at[i, :, :, rows], o_recv.at[q, 2])
            pp[i, :, rows] = add(pin[i, 0, :, rows], pin[i, 1, :, rows]).astype(BF16)
            scatter_first(i, q, lambda zz, d, r: pp.at[i, zz, r], lo, hi, 0)

    def o3(i, h):
        ring_first, rows, lo, hi = split(i, h, ROWS)
        q = i * SUB + h
        rin = ring_in.at[i]
        if ring_first:
            wait(units(4), o_recv.at[q, 1])
            quad[i, 0, rows] = add(part32[i, z, 0, rows], ring_in[i, 1, rows], ring_in[i, 2, rows]).astype(BF16)
            quad[i, 1, rows] = add(part32[i, z, 1, rows], ring_in[i, 4, rows], ring_in[i, 5, rows]).astype(BF16)
            owner_push(lambda cc: quad.at[i, cc, rows], fin.at[i, D, rows], 0, o_recv.at[q, 2])
            sent[0] += 1
            finish(lambda: wait(units(6), o_send.at[q]))
        else:
            wait(rin.at[0, rows], o_recv.at[q, 0])
            comb[i, 0, lo] = add(pin[i, 0, z1, lo], pin[i, 1, z1, lo], ring_in[i, 0, lo]).astype(BF16)
            push(comb.at[i, 0, lo], rin.at[2, lo], o_send.at[q], o_recv.at[q, 1], z_up)
            comb[i, 0, hi] = add(pin[i, 0, z3, hi], pin[i, 1, z3, hi], ring_in[i, 0, hi]).astype(BF16)
            push(comb.at[i, 0, hi], rin.at[2, hi], o_send.at[q], o_recv.at[q, 1], z_down)
            finish(lambda: wait(units(3), o_send.at[q]))

    def o4(i, h):
        ring_first, rows, lo, hi = split(i, h, ROWS)
        q = i * SUB + h
        if ring_first:
            wait(fin.at[i, :, rows], o_recv.at[q, 2])
            out_ref[i, rows] = add(fin[i, 0, rows], fin[i, 1, rows])
        else:
            wait(units(2), o_recv.at[q, 1])
            out_ref[i, rows] = add(pin[i, 0, z, rows], pin[i, 1, z, rows], ring_in[i, 1, rows], ring_in[i, 2, rows])

    at(SHARE_AT, -1, t1)
    at(SECOND_HOP, -1, t2)
    for k in range(8):
        at(k * SUB - AHEAD, -2, e1, k)
        at(k * SUB, -1, f0, k)
        for s, step in enumerate((f1, f2, f3)):
            at(k * ROW_STEP + s * ROW_LAG, s, step, k)
    rows_done = 7 * ROW_STEP + 2 * ROW_LAG + 2
    at(rows_done, 9, f4)
    at(8 * SUB, 31, e_end)
    done = {}
    amps_at = None
    for place, k in enumerate(ORDER):
        lag, parts = (FACTOR_LAG, 1) if k < 8 else (AMP_LAG, SUB)
        if k >= 8 and amps_at is None:
            amps_at = place * SUB
            at(amps_at, 3, t3)
        for h in range(parts):
            start = place * SUB + h
            for s, step in enumerate((s1, s2, s3, s4)):
                at(start + s * lag, 4 + s, step, k, h, 128 // parts, k if k < 8 else 8 + (k - 8) * SUB + h)
        done[k] = place * SUB + parts - 1 + 3 * lag + CORE_LAG
        if k >= 8:
            at(done[k], 8, amps_in, k)
    columns_done = max(done[k] for k in range(8))
    at(columns_done, 8, columns_in)
    last = 0
    for group in GROUPS:
        when = max(rows_done, last)
        for slot, i in enumerate(group):
            when = max(when, done[8 + i])
            at(when, 10, halfway, i, slot)
            when += 1
        when = max(when, columns_done)
        at(when, 10, ladder, group, 0)
        last = when + 1
        at(last, 10, ladder, group, 1)
        for i in group:
            for h in range(SUB):
                for s, step in enumerate((o1, o2, o3, o4)):
                    at(last + OUT_LAG * s, 11 + s, step, i, h)
    at(1000, 40, q_end)
    while plan:
        now[0], _, _, step, args = heapq.heappop(plan)
        step(*args)


def shards(amplitudes, df_factor, amp_mask, factor_mask):
    vmem, smem = pl.BlockSpec(memory_space=pltpu.VMEM), pl.BlockSpec(memory_space=pltpu.SMEM)
    block = lambda *lead: pltpu.VMEM((*lead, 128, 256), BF16)
    dma = lambda *shape: pltpu.SemaphoreType.DMA(shape)
    return pl.pallas_call(
        kernel,
        out_shape=jax.ShapeDtypeStruct((8, 128, 256), F32),
        in_specs=[vmem, vmem, smem, smem],
        out_specs=vmem,
        scratch_shapes=[
            pltpu.VMEM((4, 2, 8, 16, 256), BF16),
            pltpu.VMEM((4, 8, 32, 256), BF16),
            block(8),
            block(16, 4, 2, 2),
            block(8, 4, 2),
            pltpu.VMEM((8, 256, 256), BF16),
            block(8, 4, 2),
            pltpu.VMEM((8, 4, 2, 128, 256), F32),
            block(8, 6),
            block(8, 2),
            block(8, 2),
            block(8, 2),
            block(8, 2, 4),
            block(8, 4),
            dma(8 + 8 * SUB, 3), dma(8 + 8 * SUB), dma(9), dma(8, 3), dma(1), dma(8), dma(2), dma(2), dma(3),
            dma(8 * SUB, 3), dma(8 * SUB), dma(2, 2),
        ],
        compiler_params=pltpu.CompilerParams(collective_id=0, has_side_effects=True, vmem_limit_bytes=60 * 2**20),
        cost_estimate=pl.CostEstimate(flops=17179869184, bytes_accessed=4 * 2**20, transcendentals=0),
    )(amplitudes, df_factor, amp_mask, factor_mask)


def solution(mesh):
    return jax.shard_map(
        shards,
        mesh=mesh,
        in_specs=(P(None, ("wide", "narrow"), None), P(None, "wide", "narrow"), P(), P()),
        out_specs=P(None, "wide", "narrow"),
        check_vma=False,
    )
```

```python
import functools
import heapq

import jax
import jax.numpy as jnp
from jax import lax
from jax.experimental import pallas as pl
from jax.experimental.pallas import tpu as pltpu
from jax.sharding import PartitionSpec as P

MESH = pl.DeviceIdType.MESH
BF16 = jnp.bfloat16
F32 = jnp.float32
TRANSPOSED = (((1,), (1,)), ((), ()))

SUB = 2
ROWS = 128 // SUB
FACTOR_LAG = 3.5
AMP_LAG = 3.0
CORE_LAG = 1.0
OUT_LAG = 5.0
AHEAD = 6
SHARE_AT = 0.0
END_LAG = 8.0
RING_FIRST = (1, 3, 5, 7)
ROW_RING_FIRST = (1, 4, 6)
ROW_STEP = 2.0
ROW_LAG = 6.0
SECOND_HOP = 10.0
ORDER = (0, 1, 2, 3, 4, 5, 6, 7, 8, 9, 10, 11, 12, 13, 14, 15)
GROUPS = ((0, 1), (2, 3), (4, 5), (6, 7))


def kernel(amp_ref, fac_ref, amask, fmask, out_ref, tsrc, tmid, fsrc, g2, fr, half, part, part32, ring_in, comb, quad, fin, pin, pp,
           g_recv, g_send, core_recv, f_recv, f_all, f_send, e_send, a_recv, a_send, o_recv, o_send, q_send):
    w, n = lax.axis_index("wide"), lax.axis_index("narrow")
    y, x = w // 4, w % 4
    z, c = n // 2, n % 2
    A, xl = x // 2, x % 2
    D = ((x + 1) // 2) % 2
    up = lambda v, s: lax.rem(v + s + 4, 4)
    x_of = lambda a, d: a * 3 + d * (1 - 2 * a)
    dev = lambda yy, xx, zz, cc: (yy * 4 + xx, zz * 2 + cc)
    z1, z2, z3 = up(z, 1), up(z, 2), up(z, 3)
    y1, y2, y3 = up(y, 1), up(y, 2), up(y, 3)
    z_up, z_down = dev(y, x, z1, c), dev(y, x, z3, c)
    y_up, y_down = dev(y1, x, z, c), dev(y3, x, z, c)
    a_pair = dev(y, x_of(1 - A, D), z, c)
    d_pair = dev(y, x_of(A, 1 - D), z, c)
    sibling = dev(y, x, z, 1 - c)
    on_home_chip = x == 2 * A + c

    def push(src, dst, send, recv, to):
        pltpu.make_async_remote_copy(src_ref=src, dst_ref=dst, send_sem=send, recv_sem=recv, device_id=to, device_id_type=MESH).start()

    def push_or_copy(here, src, dst, send, recv, to):
        @pl.when(here)
        def _():
            pltpu.make_async_copy(src, dst, recv).start()

        @pl.when(jnp.logical_not(here))
        def _():
            push(src, dst, send, recv, to)

    def wait(ref, sem):
        pltpu.make_async_copy(ref, ref, sem).wait()

    def units(count, rows=ROWS):
        sizes = [(a, b, d, e) for a in range(1, 17) for b in range(1, 5) for d in (1, 2) for e in (1, 2) if a * b * d * e == count]
        a, b, d, e = sizes[0]
        return g2.at[pl.ds(0, a), pl.ds(0, b), pl.ds(0, d), pl.ds(0, e), pl.ds(0, rows)]

    def split(k, h, tall):
        first = h * tall
        pair_first = (k % 8 not in RING_FIRST) if tall == 128 else (h == 0 or k % 8 == 7)
        return pair_first, pl.ds(first, tall), pl.ds(first, tall // 2), pl.ds(first + tall // 2, tall // 2)

    barrier = pltpu.get_barrier_semaphore()
    for to in (sibling, d_pair, dev(y, x_of(A, 1 - D), z, 1 - c), z_up, z_down, dev(y, x, z2, c), y_up, y_down, a_pair):
        pl.semaphore_signal(barrier, inc=1, device_id=to, device_id_type=MESH)

    for h in range(2):
        keep = fmask[w, 2 * n + h].astype(F32)
        cols = pl.ds(h * 128, 128)
        fsrc[:, :, cols] = (fac_ref[:, :, cols].astype(F32) * keep).astype(BF16)
    for h in range(16):
        keep = amask[w, h].astype(F32)
        cols = pl.ds(h * 128, 128)
        tsrc[h // 4, (h // 2) % 2, :, :, pl.ds((h % 2) * 128, 128)] = (amp_ref[:, :, cols].astype(F32) * keep).astype(BF16)

    pl.semaphore_wait(barrier, 9)

    plan = []
    now = [-100.0, 0]

    def at(when, order, step, *args):
        now[1] += 1
        heapq.heappush(plan, (when, order, now[1], step, args))

    def finish(step):
        at(now[0] + END_LAG, 30, step)

    stays = [jnp.logical_and(x_of(A, d) == x, xl == c) for d in range(2)]

    def e1(k):
        for d in range(2):
            def go(d=d):
                push_or_copy(stays[d], fsrc.at[k], fr.at[k, z, c], e_send.at[d], f_recv.at[k, 0], dev(y, x_of(A, d), z, xl))

            if k in ROW_RING_FIRST:
                pl.when(c == d)(go)
            else:
                go()

    def e_end():
        for d in range(2):
            goes = jnp.logical_not(stays[d])
            pl.when(jnp.logical_and(goes, c == d))(lambda: wait(fsrc, e_send.at[d]))
            pl.when(jnp.logical_and(goes, c != d))(lambda: wait(fsrc.at[pl.ds(0, 8 - len(ROW_RING_FIRST))], e_send.at[d]))

    def t1():
        for d in range(2):
            dst = tmid.at[:, :, pl.ds(pl.multiple_of(c * 16, 16), 16)]
            push_or_copy(stays[d], tsrc.at[:, d], dst, a_send.at[d], a_recv.at[0], dev(y, x_of(A, d), z, xl))
            finish(lambda d=d: pl.when(jnp.logical_not(stays[d]))(lambda: wait(tsrc.at[:, d], a_send.at[d])))

    def t2():
        wait(tmid, a_recv.at[0])
        dst = g2.at[pl.ds(8, 8), y, A, c, pl.ds(pl.multiple_of(z * 32, 32), 32)]
        for zz in (z2, z1, z3):
            push(tmid.at[zz], dst, a_send.at[2], a_recv.at[1], dev(y, x, zz, c))
        pltpu.make_async_copy(tmid.at[z], dst, a_recv.at[1]).start()
        finish(lambda: wait(tmid.at[pl.ds(0, 3)], a_send.at[2]))

    def t3():
        wait(g2.at[pl.ds(8, 8), y, A, c], a_recv.at[1])

    def f0(k):
        wait(fr.at[k, z] if k not in ROW_RING_FIRST else fr.at[k, z, D], f_recv.at[k, 0])
        g2[k, y, A, c] = fr[k, z, D]

    def f1(k):
        pair_first = k not in ROW_RING_FIRST
        own = fr.at[k, z] if pair_first else fr.at[k, z, D]
        push(own, own, f_send.at[k], f_recv.at[k, 1], z_up)
        push(own, own, f_send.at[k], f_recv.at[k, 1], z_down)
        if not pair_first:
            push(own, own, f_send.at[k], f_all.at[0], d_pair)

    def f2(k):
        pair_first, lo, hi = k not in ROW_RING_FIRST, pl.ds(0, 64), pl.ds(64, 64)
        wait(units(4 if pair_first else 2, 128), f_recv.at[k, 1])
        if pair_first:
            push(fr.at[k, z3, 0], fr.at[k, z3, 0], f_send.at[k], f_all.at[0], z_up)
            push(fr.at[k, z1, 1], fr.at[k, z1, 1], f_send.at[k], f_all.at[0], z_down)
        else:
            push(fr.at[k, z3, D, lo], fr.at[k, z3, D, lo], f_send.at[k], f_recv.at[k, 2], z_up)
            push(fr.at[k, z1, D, hi], fr.at[k, z1, D, hi], f_send.at[k], f_recv.at[k, 2], z_down)
            push(fr.at[k, z3, D], fr.at[k, z3, D], f_send.at[k], f_all.at[0], d_pair)
            push(fr.at[k, z1, D], fr.at[k, z1, D], f_send.at[k], f_all.at[0], d_pair)

    def f3(k):
        pair_first, lo, hi = k not in ROW_RING_FIRST, pl.ds(0, 64), pl.ds(64, 64)
        if not pair_first:
            wait(fr.at[k, z2, D], f_recv.at[k, 2])
            push(fr.at[k, z2, D], fr.at[k, z2, D], f_send.at[k], f_all.at[0], d_pair)
        finish(lambda: wait(units(6 if pair_first else 7, 128), f_send.at[k]))

    def f4():
        wait(units(2 * (8 - len(ROW_RING_FIRST)) + 4 * len(ROW_RING_FIRST), 128), f_all.at[0])

    def s1(k, h, tall, at_sem):
        pair_first, rows, _, _ = split(k, h, tall)
        own = g2.at[k, y, A, c, rows]
        push(own, own, g_send.at[at_sem], g_recv.at[at_sem, 2], a_pair)
        if not pair_first:
            push(own, own, g_send.at[at_sem], g_recv.at[at_sem, 0], y_up)
            push(own, own, g_send.at[at_sem], g_recv.at[at_sem, 0], y_down)

    def s2(k, h, tall, at_sem):
        pair_first, rows, lo, hi = split(k, h, tall)
        send, recv = g_send.at[at_sem], g_recv.at[at_sem]
        if pair_first:
            wait(g2.at[k, y, 1 - A, c, rows], recv.at[2])
            own = g2.at[k, y, :, c, rows]
            push(own, own, send, recv.at[0], y_up)
            push(own, own, send, recv.at[0], y_down)
        else:
            wait(units(2, tall), recv.at[0])
            b, d = g2.at[k, y3, A, c], g2.at[k, y1, A, c]
            push(b.at[lo], b.at[lo], send, recv.at[1], y_up)
            push(d.at[hi], d.at[hi], send, recv.at[1], y_down)
            push(b.at[rows], b.at[rows], send, recv.at[2], a_pair)
            push(d.at[rows], d.at[rows], send, recv.at[2], a_pair)

    def s3(k, h, tall, at_sem):
        pair_first, rows, lo, hi = split(k, h, tall)
        send, recv = g_send.at[at_sem], g_recv.at[at_sem]
        if pair_first:
            wait(units(4, tall), recv.at[0])
            b, d = g2.at[k, y3, 0, c, rows], g2.at[k, y1, 1, c, rows]
            push(b, b, send, recv.at[1], y_up)
            push(d, d, send, recv.at[1], y_down)
        else:
            b = g2.at[k, y2, A, c, rows]
            wait(b, recv.at[1])
            push(b, b, send, recv.at[2], a_pair)

    def s4(k, h, tall, at_sem):
        pair_first, rows, lo, hi = split(k, h, tall)
        if pair_first:
            wait(g2.at[k, y2, :, c, rows], g_recv.at[at_sem, 1])
        else:
            wait(g2.at[k, :, 1 - A, c, rows], g_recv.at[at_sem, 2])
        mine = g2.at[k, :, :, c, rows]
        push(mine, mine, g_send.at[at_sem], core_recv.at[0 if k < 8 else k - 7], sibling)
        finish(lambda: wait(units(15, tall), g_send.at[at_sem]))

    def columns_in():
        wait(g2.at[pl.ds(0, 8), :, :, 1 - c], core_recv.at[0])

    def amps_in(k):
        wait(g2.at[k, :, :, 1 - c], core_recv.at[k - 7])

    def halfway(i, slot):
        for q in range(2):
            acc = jnp.zeros((512, 256), F32)
            for m in range(8):
                rows = fr[pl.ds(4 * q, 4), m // 2, m % 2].reshape(512, 256)
                acc += jnp.dot(rows, g2[8 + i, m // 2, m % 2].reshape(256, 256), preferred_element_type=F32)
            half[pl.ds(4 * q, 4), pl.ds(slot * 128, 128)] = acc.astype(BF16).reshape(4, 128, 256)

    def ladder(group, q):
        tall = pl.ds(0, 128 * len(group))
        acc = jnp.zeros((128 * len(group), 1024), F32)
        for p in range(8):
            acc += lax.dot_general(half[p, tall], g2[p, pl.ds(2 * q, 2)].reshape(1024, 256), TRANSPOSED, preferred_element_type=F32)
        for h, i in enumerate(group):
            for m in range(4):
                block = acc[h * 128:(h + 1) * 128, m * 256:(m + 1) * 256]
                part32[i, 2 * q + m // 2, m % 2] = block
                part[i, 2 * q + m // 2, m % 2] = block.astype(BF16)

    add = lambda *terms: functools.reduce(lambda a, b: a + b, [t.astype(F32) for t in terms])

    owns = [jnp.logical_and(on_home_chip, c == cc) for cc in range(2)]

    def owner_push(src_of, dst, send, sem):
        for cc in range(2):
            push_or_copy(owns[cc], src_of(cc), dst, q_send.at[send, cc], sem, dev(y, 2 * A + c, z, cc))

    def q_end():
        for cc in range(2):
            for send, count in enumerate(sent):
                pl.when(jnp.logical_not(owns[cc]))(lambda: wait(units(count), q_send.at[send, cc]))

    sent = [0, 0]

    def scatter_first(i, q, block, first, second, two):
        send, rin = o_send.at[q], ring_in.at[i]
        push(block(z2, 0, first), rin.at[0, first], send, o_recv.at[q, 0], z_up)
        push(block(z2, 1, second), rin.at[two, second], send, o_recv.at[q, 0], z_down)
        push(block(z3, 0, first), rin.at[1, first], send, o_recv.at[q, 1], z_down)
        push(block(z1, 1, second), rin.at[two + 1, second], send, o_recv.at[q, 1], z_up)

    def o1(i, h):
        ring_first, rows, lo, hi = split(i, h, ROWS)
        q = i * SUB + h
        if ring_first:
            scatter_first(i, q, lambda zz, d, r: part.at[i, zz, d, r], rows, rows, 3)
        else:
            owner_push(lambda cc: part.at[i, :, cc, rows], pin.at[i, D, :, rows], 1, o_recv.at[q, 2])
            sent[1] += 4

    def o2(i, h):
        ring_first, rows, lo, hi = split(i, h, ROWS)
        q = i * SUB + h
        rin = ring_in.at[i]
        if ring_first:
            wait(units(2), o_recv.at[q, 0])
            comb[i, 0, rows] = add(part32[i, z1, 0, rows], ring_in[i, 0, rows]).astype(BF16)
            push(comb.at[i, 0, rows], rin.at[2, rows], o_send.at[q], o_recv.at[q, 1], z_up)
            comb[i, 1, rows] = add(part32[i, z3, 1, rows], ring_in[i, 3, rows]).astype(BF16)
            push(comb.at[i, 1, rows], rin.at[5, rows], o_send.at[q], o_recv.at[q, 1], z_down)
        else:
            wait(pin.at[i, :, :, rows], o_recv.at[q, 2])
            pp[i, :, rows] = add(pin[i, 0, :, rows], pin[i, 1, :, rows]).astype(BF16)
            scatter_first(i, q, lambda zz, d, r: pp.at[i, zz, r], lo, hi, 0)

    def o3(i, h):
        ring_first, rows, lo, hi = split(i, h, ROWS)
        q = i * SUB + h
        rin = ring_in.at[i]
        if ring_first:
            wait(units(4), o_recv.at[q, 1])
            quad[i, 0, rows] = add(part32[i, z, 0, rows], ring_in[i, 1, rows], ring_in[i, 2, rows]).astype(BF16)
            quad[i, 1, rows] = add(part32[i, z, 1, rows], ring_in[i, 4, rows], ring_in[i, 5, rows]).astype(BF16)
            owner_push(lambda cc: quad.at[i, cc, rows], fin.at[i, D, rows], 0, o_recv.at[q, 2])
            sent[0] += 1
            finish(lambda: wait(units(6), o_send.at[q]))
        else:
            wait(rin.at[0, rows], o_recv.at[q, 0])
            comb[i, 0, lo] = add(pin[i, 0, z1, lo], pin[i, 1, z1, lo], ring_in[i, 0, lo]).astype(BF16)
            push(comb.at[i, 0, lo], rin.at[2, lo], o_send.at[q], o_recv.at[q, 1], z_up)
            comb[i, 0, hi] = add(pin[i, 0, z3, hi], pin[i, 1, z3, hi], ring_in[i, 0, hi]).astype(BF16)
            push(comb.at[i, 0, hi], rin.at[2, hi], o_send.at[q], o_recv.at[q, 1], z_down)
            finish(lambda: wait(units(3), o_send.at[q]))

    def o4(i, h):
        ring_first, rows, lo, hi = split(i, h, ROWS)
        q = i * SUB + h
        if ring_first:
            wait(fin.at[i, :, rows], o_recv.at[q, 2])
            out_ref[i, rows] = add(fin[i, 0, rows], fin[i, 1, rows])
        else:
            wait(units(2), o_recv.at[q, 1])
            out_ref[i, rows] = add(pin[i, 0, z, rows], pin[i, 1, z, rows], ring_in[i, 1, rows], ring_in[i, 2, rows])

    at(SHARE_AT, -1, t1)
    at(SECOND_HOP, -1, t2)
    for k in range(8):
        at(k * SUB - AHEAD, -2, e1, k)
        at(k * SUB, -1, f0, k)
        for s, step in enumerate((f1, f2, f3)):
            at(k * ROW_STEP + s * ROW_LAG, s, step, k)
    rows_done = 7 * ROW_STEP + 2 * ROW_LAG + 2
    at(rows_done, 9, f4)
    at(8 * SUB, 31, e_end)
    done = {}
    amps_at = None
    for place, k in enumerate(ORDER):
        lag, parts = (FACTOR_LAG, 1) if k < 8 else (AMP_LAG, SUB)
        if k >= 8 and amps_at is None:
            amps_at = place * SUB
            at(amps_at, 3, t3)
        for h in range(parts):
            start = place * SUB + h
            for s, step in enumerate((s1, s2, s3, s4)):
                at(start + s * lag, 4 + s, step, k, h, 128 // parts, k if k < 8 else 8 + (k - 8) * SUB + h)
        done[k] = place * SUB + parts - 1 + 3 * lag + CORE_LAG
        if k >= 8:
            at(done[k], 8, amps_in, k)
    columns_done = max(done[k] for k in range(8))
    at(columns_done, 8, columns_in)
    last = 0
    for group in GROUPS:
        when = max(rows_done, last)
        for slot, i in enumerate(group):
            when = max(when, done[8 + i])
            at(when, 10, halfway, i, slot)
            when += 1
        when = max(when, columns_done)
        at(when, 10, ladder, group, 0)
        last = when + 1
        at(last, 10, ladder, group, 1)
        for i in group:
            for h in range(SUB):
                for s, step in enumerate((o1, o2, o3, o4)):
                    at(last + OUT_LAG * s, 11 + s, step, i, h)
    at(1000, 40, q_end)
    while plan:
        now[0], _, _, step, args = heapq.heappop(plan)
        step(*args)


def shards(amplitudes, df_factor, amp_mask, factor_mask):
    vmem, smem = pl.BlockSpec(memory_space=pltpu.VMEM), pl.BlockSpec(memory_space=pltpu.SMEM)
    block = lambda *lead: pltpu.VMEM((*lead, 128, 256), BF16)
    dma = lambda *shape: pltpu.SemaphoreType.DMA(shape)
    return pl.pallas_call(
        kernel,
        out_shape=jax.ShapeDtypeStruct((8, 128, 256), F32),
        in_specs=[vmem, vmem, smem, smem],
        out_specs=vmem,
        scratch_shapes=[
            pltpu.VMEM((4, 2, 8, 16, 256), BF16),
            pltpu.VMEM((4, 8, 32, 256), BF16),
            block(8),
            block(16, 4, 2, 2),
            block(8, 4, 2),
            pltpu.VMEM((8, 256, 256), BF16),
            block(8, 4, 2),
            pltpu.VMEM((8, 4, 2, 128, 256), F32),
            block(8, 6),
            block(8, 2),
            block(8, 2),
            block(8, 2),
            block(8, 2, 4),
            block(8, 4),
            dma(8 + 8 * SUB, 3), dma(8 + 8 * SUB), dma(9), dma(8, 3), dma(1), dma(8), dma(2), dma(2), dma(3),
            dma(8 * SUB, 3), dma(8 * SUB), dma(2, 2),
        ],
        compiler_params=pltpu.CompilerParams(collective_id=0, has_side_effects=True, vmem_limit_bytes=60 * 2**20),
        cost_estimate=pl.CostEstimate(flops=17179869184, bytes_accessed=4 * 2**20, transcendentals=0),
    )(amplitudes, df_factor, amp_mask, factor_mask)


def solution(mesh):
    return jax.shard_map(
        shards,
        mesh=mesh,
        in_specs=(P(None, ("wide", "narrow"), None), P(None, "wide", "narrow"), P(), P()),
        out_specs=P(None, "wide", "narrow"),
        check_vma=False,
    )
```
